32 devices in a mesh: grp: 2 (over y), tile: 4 (over z), tm: 2 (over x), ch: 2 (over core).
Axes of the slice: x: 2, y: 2, z: 4, core: 2. Of those that a mesh axis runs over, the one named last changes fastest.
Arguments:
- latent: bfloat16 [8, 8, 64, 512], P(('grp', 'tm'), None, 'tile', 'ch'), parts along dimension 0, may hold values from -340 to 340
- norm_gain: float32 [512], P('ch'), may hold values from 0.1 to 1.9
- norm_shift: float32 [512], P('ch'), may hold values from -3 to 3
- kernel: bfloat16 [3, 3, 3, 512, 512], P(None, None, None, ('ch', 'tile', 'tm')), may hold values from -0.0546875 to 0.0546875
- conv_bias: float32 [512], P('ch'), may hold values from -3 to 3
- blend_profile: int32 [4], replicated, may hold values from 0 to 3
Outputs:
- decoded: bfloat16 [8, 8, 64, 512], P(('grp', 'tm'), None, 'tile', 'ch'), parts along dimension 0
The draws below stay inside these ranges and needn't reach their ends.
There are 2 independent parts, one for each index of `grp`. The reference program is written for one: setup_inputs(seed, part) draws one part's arguments, and reference() takes and returns one part's arrays. A program takes and returns all parts, laid end to end along the dimension named above; an argument that names none is the same for every part. Nothing has to cross between parts.
All inputs are finite; a program needn't handle non-finite values.
Results may differ from the reference program's by a relative error of at most 0.0038.
The reference program's roundings to bfloat16 on the way count: a program that leaves them out, or rounds other values in their place, can miss the bound.
Values may be sent and summed in bfloat16 or wider, within the bound.
No kernel may reach another device: no remote copies, remote signals or barrier semaphores. Data moves between devices by JAX's collectives and lax.ppermute only.
A program may use at most 64 MiB of HBM per device.

```python
import math
import jax
import jax.numpy as jnp
from jax import lax

CHANNELS = 512
GROUPS = 32
ROWS = 8
TW = 16
RIM = 4
FRAMES = 4
TILES = 4
WIDTH = 64


def draw_latent(key, part):
    key_base, key_cell, key_chan = jax.random.split(key, 3)
    full_shape = (FRAMES, ROWS, WIDTH, CHANNELS)
    chan_scale = jnp.exp(jax.random.uniform(key_chan, (1, 1, 1, CHANNELS), jnp.float32, -1.2, 1.2))
    cell_scale = jnp.exp(jax.random.uniform(key_cell, (FRAMES, ROWS, WIDTH, 1), jnp.float32) * math.log(10.0))
    base = jnp.clip(jax.random.normal(key_base, full_shape, jnp.float32), -4.0, 4.0)
    return (base * cell_scale * chan_scale).astype(jnp.bfloat16)


def place_ends(array, rng, smallest, high):
    longest = array.shape.index(max(array.shape))
    spots = []
    for shift in (0, 1):
        where = [jax.random.randint(jax.random.fold_in(rng, axis), (), 0, length) for axis, length in enumerate(array.shape)]
        where[longest] = (where[longest] + shift) % array.shape[longest]
        spots.append(tuple(where))
    return array.at[spots[0]].set(smallest).at[spots[1]].set(high)


def levels(key, shape, shards, smallest, largest):
    level, own = 1.0, jax.random.fold_in(key, 6)
    for dim, shards_of in shards:
        steps = jnp.exp(jax.random.uniform(jax.random.fold_in(own, dim), (shards_of,), jnp.float32, smallest / len(shards), largest / len(shards)))
        level = level * jnp.repeat(steps, shape[dim] // shards_of).reshape([-1 if axis == dim else 1 for axis in range(len(shape))])
    return level


def bell_draw(stream_key, extent, scale, reach, pieces=(), kind=jnp.bfloat16):
    result = jax.random.normal(stream_key, extent, jnp.float32) * scale
    if len(pieces) > 0:
        result = levels(stream_key, extent, pieces, -0.22, 0.18) * result
    return jnp.clip(result, min=-reach, max=reach).astype(kind)


def setup_inputs(seed: int = 0, part: int = 0) -> dict:
    splits = jax.random.split(jax.random.key(seed), 7)
    part_splits = jax.random.split(jax.random.fold_in(splits[6], part), 7)
    latent = draw_latent(jax.random.fold_in(jax.random.fold_in(splits[6], part), 71), part)
    norm_gain = jnp.clip(1.0 + 0.18 * jax.random.normal(splits[1], (CHANNELS,), jnp.float32), 0.1, 1.9)
    norm_shift = bell_draw(splits[2], (CHANNELS,), 0.5, 3.0, ((0, 2),), jnp.float32)
    kernel = bell_draw(splits[3], (3, 3, 3, CHANNELS, CHANNELS), (27 * CHANNELS) ** -0.5, 0.0546875, ((3, 16),))
    conv_bias = bell_draw(splits[4], (CHANNELS,), 0.3, 3.0, ((0, 2),), jnp.float32)
    blend_profile = place_ends(jax.random.randint(splits[5], (TILES,), 0, 4), jax.random.fold_in(splits[5], 1), 0, 3).astype(jnp.int32)
    return {"latent": latent, "norm_gain": norm_gain, "norm_shift": norm_shift, "kernel": kernel, "conv_bias": conv_bias, "blend_profile": blend_profile}


def ramp_weight(profile, position, margin):
    fraction = (position.astype(jnp.float32) + 0.5) / (2.0 * margin)
    exponent = 1.0 + profile.astype(jnp.float32)
    near_part = jnp.power(1.0 - fraction, exponent)
    far_part = jnp.power(fraction, exponent)
    return near_part / (near_part + far_part)

def frame_stats(values, colmask, groups):
    frame_count, row_count, col_count, chan_count = values.shape
    grouped = values.reshape(frame_count, row_count, col_count, groups, chan_count // groups)
    weight = colmask.reshape(1, 1, col_count, 1, 1)
    counted = row_count * (chan_count // groups) * jnp.sum(colmask)
    center = lax.optimization_barrier(jnp.sum(grouped * weight, axis=(1, 2, 4))) / counted
    spread = (grouped - center[:, None, None, :, None]) * weight
    inverse = lax.rsqrt(lax.optimization_barrier(jnp.sum(spread * spread, axis=(1, 2, 4))) / counted + 1e-06)
    return (center, inverse)

def activate(values, center, inverse, norm_gain, norm_shift, colmask, timemask, groups):
    frame_count, row_count, col_count, chan_count = values.shape
    grouped = values.reshape(frame_count, row_count, col_count, groups, chan_count // groups)
    normed = (grouped - center[:, None, None, :, None]) * inverse[:, None, None, :, None]
    normed = normed.reshape(values.shape) * norm_gain + norm_shift
    masked = jax.nn.silu(normed) * colmask[None, None, :, None] * timemask[:, None, None, None]
    return masked.astype(jnp.bfloat16)

def conv_taps(padded, kernel_part, frame_count, row_count, col_count):
    in_width = kernel_part.shape[3]
    running = None
    for tap_time in range(3):
        for tap_row in range(3):
            for tap_col in range(3):
                window = padded[tap_time:tap_time + frame_count, tap_row:tap_row + row_count, tap_col:tap_col + col_count]
                contrib = jnp.dot(window.reshape(-1, in_width), kernel_part[tap_time, tap_row, tap_col], preferred_element_type=jnp.float32)
                running = contrib if running is None else running + contrib
    return running

def reference(latent, norm_gain, norm_shift, kernel, conv_bias, blend_profile):
    cols_all = TW + 2 * RIM

    def one_tile(tile_pos):
        column = tile_pos * TW - RIM + jnp.arange(cols_all, dtype=jnp.int32)
        colmask = ((column >= 0) & (column < WIDTH)).astype(jnp.float32)
        picked = jnp.take(latent, jnp.clip(column, 0, WIDTH - 1).astype(jnp.int32), axis=2).astype(jnp.float32)
        picked = picked * colmask[None, None, :, None]
        center, inverse = frame_stats(picked, colmask, GROUPS)
        timemask = jnp.ones((FRAMES,), jnp.float32)
        activated = activate(picked, center, inverse, norm_gain, norm_shift, colmask, timemask, GROUPS)
        padded = jnp.pad(activated, ((2, 0), (1, 1), (1, 1), (0, 0)))
        running = conv_taps(padded, kernel, FRAMES, ROWS, cols_all)
        return (running.reshape(FRAMES, ROWS, cols_all, CHANNELS) + conv_bias).astype(jnp.bfloat16)
    outputs = lax.map(one_tile, jnp.arange(TILES, dtype=jnp.int32))
    own_all = outputs[:, :, :, RIM:RIM + TW].astype(jnp.float32)
    zero_tile = jnp.zeros_like(outputs[:1])
    before = jnp.concatenate([zero_tile, outputs[:-1]], axis=0)
    after = jnp.concatenate([outputs[1:], zero_tile], axis=0)
    left_nbr = before[:, :, :, TW + RIM:].astype(jnp.float32)
    right_nbr = after[:, :, :, :RIM].astype(jnp.float32)
    tile_ids = jnp.arange(TILES, dtype=jnp.int32)
    offsets = jnp.arange(RIM, dtype=jnp.int32)
    prev_profile = jnp.concatenate([blend_profile[:1], blend_profile[:-1]])
    left_weight = jnp.where(tile_ids[:, None] > 0, ramp_weight(prev_profile[:, None], offsets[None, :] + RIM, RIM), 0.0)
    right_weight = jnp.where(tile_ids[:, None] < TILES - 1, ramp_weight(blend_profile[:, None], offsets[None, :], RIM), 1.0)
    left_wide = left_weight[:, None, None, :, None]
    right_wide = right_weight[:, None, None, :, None]
    head_cols = own_all[:, :, :, :RIM] * (1.0 - left_wide) + left_nbr * left_wide
    tail_cols = own_all[:, :, :, TW - RIM:] * right_wide + right_nbr * (1.0 - right_wide)
    middle = own_all[:, :, :, RIM:TW - RIM]
    core_all = jnp.concatenate([head_cols, middle, tail_cols], axis=3)
    return jnp.moveaxis(core_all, 0, 2).reshape(FRAMES, ROWS, WIDTH, CHANNELS).astype(jnp.bfloat16)
```

```python
import functools

import jax
import jax.numpy as jnp
from jax import lax
from jax.experimental import pallas as pl
from jax.experimental.pallas import tpu as pltpu
from jax.sharding import PartitionSpec as P

GROUPS = 32
RIM = 4
TAPS = 3


def ramp_weight(profile, position, margin):
    fraction = (position.astype(jnp.float32) + 0.5) / (2.0 * margin)
    exponent = 1.0 + profile.astype(jnp.float32)
    near_part = jnp.power(1.0 - fraction, exponent)
    far_part = jnp.power(fraction, exponent)
    return near_part / (near_part + far_part)


def with_halo(shard, sides, width):
    for axis, dim in sides:
        size, length = (lax.axis_size(axis), shard.shape[dim])
        up = [(i, (i + 1) % size) for i in range(size - 1)]
        down = [(j, i) for i, j in up]
        last = lax.slice_in_dim(shard, length - width, length, axis=dim)
        leading = lax.slice_in_dim(shard, 0, width, axis=dim)
        before = lax.ppermute(last, axis, up)
        after = lax.ppermute(leading, axis, down)
        shard = jnp.concatenate([before, shard, after], axis=dim)
    return shard


def passed_along(block, axis, distance):
    devices = range(lax.axis_size(axis))
    route = [(i - distance, i) for i in devices if i - distance in devices]
    return lax.ppermute(block, axis, route)


def frame_stats(values, colmask, groups):
    frame_count, row_count, col_count, chan_count = values.shape
    grouped = values.reshape(frame_count, row_count, col_count, groups, chan_count // groups)
    weight = colmask.reshape(1, 1, col_count, 1, 1)
    counted = row_count * (chan_count // groups) * jnp.sum(colmask)
    center = jnp.sum(grouped * weight, axis=(1, 2, 4)) / counted
    spread = (grouped - center[:, None, None, :, None]) * weight
    inverse = lax.rsqrt(jnp.sum(spread * spread, axis=(1, 2, 4)) / counted + 1e-06)
    return (center, inverse)


def activate(values, center, inverse, norm_gain, norm_shift, colmask, timemask, groups):
    frame_count, row_count, col_count, chan_count = values.shape
    grouped = values.reshape(frame_count, row_count, col_count, groups, chan_count // groups)
    normed = (grouped - center[:, None, None, :, None]) * inverse[:, None, None, :, None]
    normed = normed.reshape(values.shape) * norm_gain + norm_shift
    masked = jax.nn.silu(normed) * colmask[None, None, :, None] * timemask[:, None, None, None]
    return masked.astype(jnp.bfloat16)


def conv_taps(padded, kernel_part, frame_count, row_count, col_count):
    in_width = kernel_part.shape[3]
    running = None
    for tap_time in range(3):
        for tap_row in range(3):
            for tap_col in range(3):
                window = padded[
                    tap_time : tap_time + frame_count,
                    tap_row : tap_row + row_count,
                    tap_col : tap_col + col_count,
                ]
                contrib = jnp.dot(
                    window.reshape(-1, in_width),
                    kernel_part[tap_time, tap_row, tap_col],
                    preferred_element_type=jnp.float32,
                )
                running = contrib if running is None else running + contrib
    return running


def gathered_plan(latent, norm_gain, norm_shift, kernel, conv_bias, blend_profile):
    frame_count, row_count, core_cols, chan_half = latent.shape
    out_chans = kernel.shape[4]
    groups = GROUPS // lax.axis_size("ch")
    ncols = core_cols + 2 * RIM
    tile_pos = lax.axis_index("tile")
    tile_count = lax.axis_size("tile")
    window_in = with_halo(latent, (("tile", 2),), RIM)
    cached = passed_along(window_in, "tm", 1)
    frames = jnp.concatenate([cached, window_in], axis=0).astype(jnp.float32)
    column = tile_pos * core_cols - RIM + jnp.arange(ncols, dtype=jnp.int32)
    colmask = ((column >= 0) & (column < tile_count * core_cols)).astype(jnp.float32)
    started = (lax.axis_index("tm") > 0).astype(jnp.float32)
    timemask = jnp.concatenate(
        [jnp.ones((2,), jnp.float32) * started, jnp.ones((frame_count,), jnp.float32)]
    )
    center, inverse = frame_stats(frames, colmask, groups)
    activated = activate(frames, center, inverse, norm_gain, norm_shift, colmask, timemask, groups)
    padded = jnp.pad(activated, ((0, 0), (1, 1), (1, 1), (0, 0)))
    whole_kernel = lax.all_gather(kernel, ("tile", "tm"), axis=3, tiled=True)
    running = conv_taps(padded, whole_kernel, frame_count, row_count, ncols)
    joined = running.reshape(frame_count, row_count, ncols, out_chans)
    summed = lax.psum_scatter(joined, "ch", scatter_dimension=3, tiled=True)
    tile_out = (summed + conv_bias).astype(jnp.bfloat16)
    extended = with_halo(tile_out, (("tile", 2),), RIM)
    own_out = tile_out[:, :, RIM : RIM + core_cols]
    left_nbr = extended[:, :, :RIM]
    right_nbr = extended[:, :, ncols + RIM :]
    own_profile = lax.dynamic_index_in_dim(blend_profile, tile_pos, 0, keepdims=False)
    prev_profile = lax.dynamic_index_in_dim(
        blend_profile, jnp.maximum(tile_pos - 1, 0), 0, keepdims=False
    )
    offsets = jnp.arange(RIM, dtype=jnp.int32)
    left_weight = jnp.where(tile_pos > 0, ramp_weight(prev_profile, offsets + RIM, RIM), 0.0)
    right_weight = jnp.where(tile_pos < tile_count - 1, ramp_weight(own_profile, offsets, RIM), 1.0)
    left_wide = left_weight[None, None, :, None]
    right_wide = right_weight[None, None, :, None]
    own_float = own_out.astype(jnp.float32)
    head_cols = own_float[:, :, :RIM] * (1.0 - left_wide) + left_nbr.astype(jnp.float32) * left_wide
    tail_cols = own_float[:, :, core_cols - RIM :] * right_wide + right_nbr.astype(jnp.float32) * (
        1.0 - right_wide
    )
    middle = own_float[:, :, RIM : core_cols - RIM]
    return jnp.concatenate([head_cols, middle, tail_cols], axis=2).astype(jnp.bfloat16)


VMEM_BYTES = 48 * 1024 * 1024


def resident_fits(mesh, latent, kernel):
    return (
        mesh["tile"] == 4
        and mesh["tm"] == 2
        and mesh["ch"] == 2
        and latent.shape == (2, 8, 16, 256)
        and kernel.shape == (TAPS, TAPS, TAPS, 32, 512)
    )


def call(body, outs, scratch=(), smem_first=True):
    vmem = pl.BlockSpec(memory_space=pltpu.VMEM)
    smem = pl.BlockSpec(memory_space=pltpu.SMEM)

    def run(*args):
        specs = [smem if smem_first and i == 0 else vmem for i in range(len(args))]
        return pl.pallas_call(
            body,
            out_shape=outs,
            in_specs=specs,
            out_specs=jax.tree.map(lambda _: vmem, outs),
            scratch_shapes=list(scratch),
            compiler_params=pltpu.CompilerParams(vmem_limit_bytes=VMEM_BYTES),
        )(*args)

    return run


def pack_body(pos, latent, *outs):
    z = pos[0]
    first = latent[0].astype(jnp.float32)
    second = latent[1].astype(jnp.float32)
    for owner in range(4):
        lanes = slice(64 * owner, 64 * owner + 64)
        block = jnp.concatenate([first[..., lanes], second[..., lanes]], axis=-1)
        block = block.astype(jnp.bfloat16)
        for k in range(4):

            @pl.when(z == owner ^ k)
            def _():
                outs[k][...] = block


def group_sum(rows):
    lane = lax.broadcasted_iota(jnp.int32, rows.shape, 1)
    for step in (1, 2, 4, 8):
        ahead = pltpu.roll(rows, 128 - step, 1)
        behind = pltpu.roll(rows, step, 1)
        rows = rows + jnp.where((lane & step) == 0, ahead, behind)
    return rows


def norm_body(pos, gain, shift, *refs):
    blocks, (out, placed, raw) = refs[:8], refs[8:]
    z, x = pos[0], pos[1]
    for k in range(4):
        placed[x, z ^ k] = blocks[k][...]
        placed[1 - x, z ^ k] = blocks[4 + k][...]
    for p in range(2):
        raw[p, :, 0:4, :] = jnp.zeros((8, 4, 128), jnp.float32)
        raw[p, :, 68:72, :] = jnp.zeros((8, 4, 128), jnp.float32)
        for t in range(4):
            raw[p, :, 4 + 16 * t : 20 + 16 * t, :] = placed[p, t].astype(jnp.float32)
    col = lax.broadcasted_iota(jnp.int32, (24, 128), 0)
    present = {0: col >= 4, 3: col < 20}
    count_row = lax.broadcasted_iota(jnp.int32, (8, 128), 0) % 4
    cells = jnp.where((count_row == 0) | (count_row == 3), 20.0, 24.0) * 128.0

    def window(p, t):
        return raw[p, :, 16 * t : 16 * t + 24, :]

    sums = []
    for p in range(2):
        for t in range(4):
            over_rows = jnp.sum(window(p, t), axis=0)
            sums.append(jnp.sum(over_rows, axis=0, keepdims=True))
    center = group_sum(jnp.concatenate(sums, axis=0)) / cells
    sums = []
    for p in range(2):
        for t in range(4):
            at = 4 * p + t
            spread = window(p, t) - center[at : at + 1][None]
            over_rows = jnp.sum(spread * spread, axis=0)
            if t in present:
                over_rows = jnp.where(present[t], over_rows, 0.0)
            sums.append(jnp.sum(over_rows, axis=0, keepdims=True))
    inverse = lax.rsqrt(group_sum(jnp.concatenate(sums, axis=0)) / cells + 1e-06)
    scale = inverse * gain[...]
    offset = shift[...]
    for p in range(2):
        for half in range(2):
            acts = []
            for t in (2 * half, 2 * half + 1):
                at = 4 * p + t
                normed = (window(p, t) - center[at : at + 1][None]) * scale[at : at + 1][None]
                near = 0.5 * (normed + offset[None])
                act = near + near * jnp.tanh(near)
                if t in present:
                    act = jnp.where(present[t][None], act, 0.0)
                acts.append(act)
            joined = jnp.concatenate(acts, axis=1).astype(jnp.bfloat16)
            out[p, :, 48 * half : 48 * half + 48, :] = joined


def weights_body(pos, same, other, same_far, other_far, diag, lower):
    x = pos[1]
    zero = jnp.zeros((32, 128), jnp.bfloat16)
    for b in range(TAPS):
        for e in range(TAPS):
            for core, (near, far) in enumerate(((same, same_far), (other, other_far))):
                for f in range(2):
                    base = e * 256 + core * 128 + f * 64
                    for g in range(2):
                        tap_d, tap_l = f - g + 2, f - g
                        for source, slot in ((near, x), (far, 1 - x)):
                            rows = pl.ds(pl.multiple_of(base + 32 * slot, 32), 32)
                            lanes = slice(128 * g, 128 * g + 128)
                            diag[b, rows, lanes] = source[tap_d, b, e] if tap_d < 3 else zero
                            lower[b, rows, lanes] = source[tap_l, b, e] if tap_l >= 0 else zero


def conv_body(pos, mine, sibling, diag, lower, blend, *refs):
    own, sends, (stacked, summed, blocks) = refs[0], refs[1:8], refs[8:]
    z, x = pos[0], pos[1]
    col = lax.broadcasted_iota(jnp.int32, (24, 128), 0)
    for p in range(2):
        edge = jnp.zeros((96, 768), jnp.bfloat16)
        stacked[p, 0:96, :] = edge
        stacked[p, 864:960, :] = edge
        for core, source in enumerate((mine, sibling)):
            act = source[p].reshape(768, 128)
            wide = act.astype(jnp.float32)
            before = pltpu.roll(wide, 1, 0).reshape(32, 24, 128)
            before = jnp.where((col > 0)[None], before, 0.0).reshape(768, 128)
            after = pltpu.roll(wide, 767, 0).reshape(32, 24, 128)
            after = jnp.where((col < 23)[None], after, 0.0).reshape(768, 128)
            lanes = 128 * core
            stacked[p, 96:864, lanes : lanes + 128] = before.astype(jnp.bfloat16)
            stacked[p, 96:864, 256 + lanes : 384 + lanes] = act
            stacked[p, 96:864, 512 + lanes : 640 + lanes] = after.astype(jnp.bfloat16)

    def product(p, b, matrix):
        rows = stacked[p, 96 * b : 96 * b + 768, :]
        return jnp.dot(rows, matrix[b], preferred_element_type=jnp.float32)

    for p in range(2):
        total = sum(product(p, b, diag) for b in range(TAPS))
        if p == 1:
            total = total + sum(product(0, b, lower) for b in range(TAPS))
        total = total.reshape(8, 96, 256)
        for t in range(4):
            start = 24 * t
            left = total[:, start : start + 8]
            if t > 0:
                share = blend[t - 1][None]
                left = share * total[:, start - 8 : start] + (1.0 - share) * left
            summed[:, 16 * t : 16 * t + 8, :] = left
            summed[:, 16 * t + 8 : 16 * t + 16, :] = total[:, start + 8 : start + 16]
        summed[:, 64:72, :] = total[:, 88:96]
        for t in range(4):
            blocks[p, t] = summed[:, 4 + 16 * t : 20 + 16 * t, :]
    own[...] = blocks[x, z]
    for k in range(1, 4):
        sends[k - 1][...] = blocks[x, z ^ k].astype(jnp.bfloat16)
    for k in range(4):
        sends[3 + k][...] = blocks[1 - x, z ^ k].astype(jnp.bfloat16)


def join_body(pos, bias, own, *refs):
    same, far, out = refs[:3], refs[3:7], refs[7]
    x = pos[1]
    near_sum = own[...]
    for part in same:
        near_sum = near_sum + part[...].astype(jnp.float32)
    far_sum = far[0][...].astype(jnp.float32)
    for part in far[1:]:
        far_sum = far_sum + part[...].astype(jnp.float32)
    low = jnp.where(x == 0, near_sum, far_sum)
    high = jnp.where(x == 0, far_sum, near_sum)
    for f in range(2):
        lanes = slice(128 * f, 128 * f + 128)
        out[f, :, :, 0:128] = (low[..., lanes] + bias[:, 0:128][None]).astype(jnp.bfloat16)
        out[f, :, :, 128:256] = (high[..., lanes] + bias[:, 128:256][None]).astype(jnp.bfloat16)


def exchanged(block, k, j):
    tms = lax.axis_size("tm")
    tiles = lax.axis_size("tile")
    route = [(t * tms + m, (t ^ k) * tms + (m ^ j)) for t in range(tiles) for m in range(tms)]
    return lax.ppermute(block, ("tile", "tm"), route)


def across(block, j):
    route = [(2 * m + c, 2 * (m ^ j) + (1 - c)) for m in range(2) for c in range(2)]
    return lax.ppermute(block, ("tm", "ch"), route)


def resident_plan(latent, norm_gain, norm_shift, kernel, conv_bias, blend_profile):
    bf16, f32 = jnp.bfloat16, jnp.float32
    z, x, c = lax.axis_index("tile"), lax.axis_index("tm"), lax.axis_index("ch")
    pos = jnp.stack([z, x]).astype(jnp.int32)
    block = jax.ShapeDtypeStruct((8, 16, 128), bf16)
    wide = jax.ShapeDtypeStruct((8, 16, 256), bf16)

    packed = call(pack_body, [block] * 4)(pos, latent)
    near = [packed[0]] + [exchanged(packed[k], k, 0) for k in (1, 2, 3)]
    far = [exchanged(packed[k], k, 1) for k in range(4)]

    def quarter(core, frame_block):
        start = core * 256 + frame_block * 128
        return lax.dynamic_slice_in_dim(kernel, start, 128, axis=4)

    same = quarter(c, x)
    other = across(quarter(1 - c, x), 0)
    same_far = exchanged(quarter(c, 1 - x), 0, 1)
    other_far = across(quarter(1 - c, 1 - x), 1)
    matrix = jax.ShapeDtypeStruct((TAPS, 768, 256), bf16)
    diag, lower = call(weights_body, [matrix] * 2)(pos, same, other, same_far, other_far)

    def lanes_of(vector):
        part = lax.dynamic_slice_in_dim(vector, z * 64, 64)
        return jnp.concatenate([part, part])[None]

    acts = call(
        norm_body,
        jax.ShapeDtypeStruct((2, 8, 96, 128), bf16),
        [pltpu.VMEM((2, 4, 8, 16, 128), bf16), pltpu.VMEM((2, 8, 72, 128), f32)],
    )(pos, lanes_of(norm_gain), lanes_of(norm_shift), *near, *far)
    sibling = lax.ppermute(acts, "ch", [(0, 1), (1, 0)])

    offsets = jnp.arange(2 * RIM, dtype=jnp.int32)
    ramps = ramp_weight(blend_profile[:3, None], offsets[None, :], RIM)
    blend = jnp.broadcast_to(ramps[:, :, None], (3, 2 * RIM, 256))
    own, *sends = call(
        conv_body,
        [jax.ShapeDtypeStruct((8, 16, 256), f32)] + [wide] * 7,
        [
            pltpu.VMEM((2, 960, 768), bf16),
            pltpu.VMEM((8, 72, 256), f32),
            pltpu.VMEM((2, 4, 8, 16, 256), f32),
        ],
    )(pos, acts, sibling, diag, lower, blend)
    near_sums = [exchanged(sends[k - 1], k, 0) for k in (1, 2, 3)]
    far_sums = [exchanged(sends[3 + k], k, 1) for k in range(4)]
    return call(join_body, jax.ShapeDtypeStruct(latent.shape, bf16))(
        pos, conv_bias[None], own, *near_sums, *far_sums
    )


def solution(mesh):
    in_specs = (
        P(("grp", "tm"), None, "tile", "ch"),
        P("ch"),
        P("ch"),
        P(None, None, None, ("ch", "tile", "tm"), None),
        P("ch"),
        P(),
    )
    out_specs = P(("grp", "tm"), None, "tile", "ch")

    def on_device(latent, norm_gain, norm_shift, kernel, conv_bias, blend_profile):
        plan = resident_plan if resident_fits(mesh.shape, latent, kernel) else gathered_plan
        return plan(latent, norm_gain, norm_shift, kernel, conv_bias, blend_profile)

    return jax.shard_map(
        on_device, mesh=mesh, in_specs=in_specs, out_specs=out_specs, check_vma=False
    )
```

```python
import functools

import jax
import jax.numpy as jnp
from jax import lax
from jax.experimental import pallas as pl
from jax.experimental.pallas import tpu as pltpu
from jax.sharding import PartitionSpec as P

GROUPS = 32
RIM = 4
TAPS = 3


def ramp_weight(profile, position, margin):
    fraction = (position.astype(jnp.float32) + 0.5) / (2.0 * margin)
    exponent = 1.0 + profile.astype(jnp.float32)
    near_part = jnp.power(1.0 - fraction, exponent)
    far_part = jnp.power(fraction, exponent)
    return near_part / (near_part + far_part)


def with_halo(shard, sides, width):
    for axis, dim in sides:
        size, length = (lax.axis_size(axis), shard.shape[dim])
        up = [(i, (i + 1) % size) for i in range(size - 1)]
        down = [(j, i) for i, j in up]
        last = lax.slice_in_dim(shard, length - width, length, axis=dim)
        leading = lax.slice_in_dim(shard, 0, width, axis=dim)
        before = lax.ppermute(last, axis, up)
        after = lax.ppermute(leading, axis, down)
        shard = jnp.concatenate([before, shard, after], axis=dim)
    return shard


def passed_along(block, axis, distance):
    devices = range(lax.axis_size(axis))
    route = [(i - distance, i) for i in devices if i - distance in devices]
    return lax.ppermute(block, axis, route)


def frame_stats(values, colmask, groups):
    frame_count, row_count, col_count, chan_count = values.shape
    grouped = values.reshape(frame_count, row_count, col_count, groups, chan_count // groups)
    weight = colmask.reshape(1, 1, col_count, 1, 1)
    counted = row_count * (chan_count // groups) * jnp.sum(colmask)
    center = jnp.sum(grouped * weight, axis=(1, 2, 4)) / counted
    spread = (grouped - center[:, None, None, :, None]) * weight
    inverse = lax.rsqrt(jnp.sum(spread * spread, axis=(1, 2, 4)) / counted + 1e-06)
    return (center, inverse)


def activate(values, center, inverse, norm_gain, norm_shift, colmask, timemask, groups):
    frame_count, row_count, col_count, chan_count = values.shape
    grouped = values.reshape(frame_count, row_count, col_count, groups, chan_count // groups)
    normed = (grouped - center[:, None, None, :, None]) * inverse[:, None, None, :, None]
    normed = normed.reshape(values.shape) * norm_gain + norm_shift
    masked = jax.nn.silu(normed) * colmask[None, None, :, None] * timemask[:, None, None, None]
    return masked.astype(jnp.bfloat16)


def conv_taps(padded, kernel_part, frame_count, row_count, col_count):
    in_width = kernel_part.shape[3]
    running = None
    for tap_time in range(3):
        for tap_row in range(3):
            for tap_col in range(3):
                window = padded[
                    tap_time : tap_time + frame_count,
                    tap_row : tap_row + row_count,
                    tap_col : tap_col + col_count,
                ]
                contrib = jnp.dot(
                    window.reshape(-1, in_width),
                    kernel_part[tap_time, tap_row, tap_col],
                    preferred_element_type=jnp.float32,
                )
                running = contrib if running is None else running + contrib
    return running


def gathered_plan(latent, norm_gain, norm_shift, kernel, conv_bias, blend_profile):
    frame_count, row_count, core_cols, chan_half = latent.shape
    out_chans = kernel.shape[4]
    groups = GROUPS // lax.axis_size("ch")
    ncols = core_cols + 2 * RIM
    tile_pos = lax.axis_index("tile")
    tile_count = lax.axis_size("tile")
    window_in = with_halo(latent, (("tile", 2),), RIM)
    cached = passed_along(window_in, "tm", 1)
    frames = jnp.concatenate([cached, window_in], axis=0).astype(jnp.float32)
    column = tile_pos * core_cols - RIM + jnp.arange(ncols, dtype=jnp.int32)
    colmask = ((column >= 0) & (column < tile_count * core_cols)).astype(jnp.float32)
    started = (lax.axis_index("tm") > 0).astype(jnp.float32)
    timemask = jnp.concatenate(
        [jnp.ones((2,), jnp.float32) * started, jnp.ones((frame_count,), jnp.float32)]
    )
    center, inverse = frame_stats(frames, colmask, groups)
    activated = activate(frames, center, inverse, norm_gain, norm_shift, colmask, timemask, groups)
    padded = jnp.pad(activated, ((0, 0), (1, 1), (1, 1), (0, 0)))
    whole_kernel = lax.all_gather(kernel, ("tile", "tm"), axis=3, tiled=True)
    running = conv_taps(padded, whole_kernel, frame_count, row_count, ncols)
    joined = running.reshape(frame_count, row_count, ncols, out_chans)
    summed = lax.psum_scatter(joined, "ch", scatter_dimension=3, tiled=True)
    tile_out = (summed + conv_bias).astype(jnp.bfloat16)
    extended = with_halo(tile_out, (("tile", 2),), RIM)
    own_out = tile_out[:, :, RIM : RIM + core_cols]
    left_nbr = extended[:, :, :RIM]
    right_nbr = extended[:, :, ncols + RIM :]
    own_profile = lax.dynamic_index_in_dim(blend_profile, tile_pos, 0, keepdims=False)
    prev_profile = lax.dynamic_index_in_dim(
        blend_profile, jnp.maximum(tile_pos - 1, 0), 0, keepdims=False
    )
    offsets = jnp.arange(RIM, dtype=jnp.int32)
    left_weight = jnp.where(tile_pos > 0, ramp_weight(prev_profile, offsets + RIM, RIM), 0.0)
    right_weight = jnp.where(tile_pos < tile_count - 1, ramp_weight(own_profile, offsets, RIM), 1.0)
    left_wide = left_weight[None, None, :, None]
    right_wide = right_weight[None, None, :, None]
    own_float = own_out.astype(jnp.float32)
    head_cols = own_float[:, :, :RIM] * (1.0 - left_wide) + left_nbr.astype(jnp.float32) * left_wide
    tail_cols = own_float[:, :, core_cols - RIM :] * right_wide + right_nbr.astype(jnp.float32) * (
        1.0 - right_wide
    )
    middle = own_float[:, :, RIM : core_cols - RIM]
    return jnp.concatenate([head_cols, middle, tail_cols], axis=2).astype(jnp.bfloat16)


VMEM_BYTES = 48 * 1024 * 1024


def resident_fits(mesh, latent, kernel):
    return (
        mesh["tile"] == 4
        and mesh["tm"] == 2
        and mesh["ch"] == 2
        and latent.shape == (2, 8, 16, 256)
        and kernel.shape == (TAPS, TAPS, TAPS, 32, 512)
    )


def call(body, outs, scratch=(), smem_first=True):
    vmem = pl.BlockSpec(memory_space=pltpu.VMEM)
    smem = pl.BlockSpec(memory_space=pltpu.SMEM)

    def run(*args):
        specs = [smem if smem_first and i == 0 else vmem for i in range(len(args))]
        return pl.pallas_call(
            body,
            out_shape=outs,
            in_specs=specs,
            out_specs=jax.tree.map(lambda _: vmem, outs),
            scratch_shapes=list(scratch),
            compiler_params=pltpu.CompilerParams(vmem_limit_bytes=VMEM_BYTES),
            cost_estimate=pl.CostEstimate(flops=1000, bytes_accessed=1000, transcendentals=0),
        )(*args)

    return run


def pack_body(pos, latent, *outs):
    z = pos[0]
    first = latent[0].astype(jnp.float32)
    second = latent[1].astype(jnp.float32)
    for owner in range(4):
        lanes = slice(64 * owner, 64 * owner + 64)
        block = jnp.concatenate([first[..., lanes], second[..., lanes]], axis=-1)
        block = block.astype(jnp.bfloat16)
        for k in range(4):

            @pl.when(z == owner ^ k)
            def _():
                outs[k][...] = block


def group_sum(rows):
    lane = lax.broadcasted_iota(jnp.int32, rows.shape, 1)
    for step in (1, 2, 4, 8):
        ahead = pltpu.roll(rows, 128 - step, 1)
        behind = pltpu.roll(rows, step, 1)
        rows = rows + jnp.where((lane & step) == 0, ahead, behind)
    return rows


def norm_body(pos, gain, shift, *refs):
    blocks, (out, placed, raw) = refs[:8], refs[8:]
    z, x = pos[0], pos[1]
    for k in range(4):
        placed[x, z ^ k] = blocks[k][...]
        placed[1 - x, z ^ k] = blocks[4 + k][...]
    for p in range(2):
        raw[p, :, 0:4, :] = jnp.zeros((8, 4, 128), jnp.float32)
        raw[p, :, 68:72, :] = jnp.zeros((8, 4, 128), jnp.float32)
        for t in range(4):
            raw[p, :, 4 + 16 * t : 20 + 16 * t, :] = placed[p, t].astype(jnp.float32)
    col = lax.broadcasted_iota(jnp.int32, (24, 128), 0)
    present = {0: col >= 4, 3: col < 20}
    count_row = lax.broadcasted_iota(jnp.int32, (8, 128), 0) % 4
    cells = jnp.where((count_row == 0) | (count_row == 3), 20.0, 24.0) * 128.0

    def window(p, t):
        return raw[p, :, 16 * t : 16 * t + 24, :]

    sums = []
    for p in range(2):
        for t in range(4):
            over_rows = jnp.sum(window(p, t), axis=0)
            sums.append(jnp.sum(over_rows, axis=0, keepdims=True))
    center = group_sum(jnp.concatenate(sums, axis=0)) / cells
    sums = []
    for p in range(2):
        for t in range(4):
            at = 4 * p + t
            spread = window(p, t) - center[at : at + 1][None]
            over_rows = jnp.sum(spread * spread, axis=0)
            if t in present:
                over_rows = jnp.where(present[t], over_rows, 0.0)
            sums.append(jnp.sum(over_rows, axis=0, keepdims=True))
    inverse = lax.rsqrt(group_sum(jnp.concatenate(sums, axis=0)) / cells + 1e-06)
    scale = inverse * gain[...]
    offset = shift[...]
    for p in range(2):
        for half in range(2):
            acts = []
            for t in (2 * half, 2 * half + 1):
                at = 4 * p + t
                normed = (window(p, t) - center[at : at + 1][None]) * scale[at : at + 1][None]
                near = 0.5 * (normed + offset[None])
                act = near + near * jnp.tanh(near)
                if t in present:
                    act = jnp.where(present[t][None], act, 0.0)
                acts.append(act)
            joined = jnp.concatenate(acts, axis=1).astype(jnp.bfloat16)
            out[p, :, 48 * half : 48 * half + 48, :] = joined


def weights_body(pos, same, other, same_far, other_far, diag, lower):
    x = pos[1]
    zero = jnp.zeros((32, 128), jnp.bfloat16)
    for b in range(TAPS):
        for e in range(TAPS):
            for core, (near, far) in enumerate(((same, same_far), (other, other_far))):
                for f in range(2):
                    base = e * 256 + core * 128 + f * 64
                    for g in range(2):
                        tap_d, tap_l = f - g + 2, f - g
                        for source, slot in ((near, x), (far, 1 - x)):
                            rows = pl.ds(pl.multiple_of(base + 32 * slot, 32), 32)
                            lanes = slice(128 * g, 128 * g + 128)
                            diag[b, rows, lanes] = source[tap_d, b, e] if tap_d < 3 else zero
                            lower[b, rows, lanes] = source[tap_l, b, e] if tap_l >= 0 else zero


def conv_body(pos, mine, sibling, diag, lower, blend, *refs):
    own, sends, kept, passed, (stacked, summed, blocks) = refs[0], refs[1:4], refs[4], refs[5], refs[6:]
    z, x = pos[0], pos[1]
    col = lax.broadcasted_iota(jnp.int32, (24, 128), 0)
    for p in range(2):
        edge = jnp.zeros((96, 768), jnp.bfloat16)
        stacked[p, 0:96, :] = edge
        stacked[p, 864:960, :] = edge
        for core, source in enumerate((mine, sibling)):
            act = source[p].reshape(768, 128)
            wide = act.astype(jnp.float32)
            before = pltpu.roll(wide, 1, 0).reshape(32, 24, 128)
            before = jnp.where((col > 0)[None], before, 0.0).reshape(768, 128)
            after = pltpu.roll(wide, 767, 0).reshape(32, 24, 128)
            after = jnp.where((col < 23)[None], after, 0.0).reshape(768, 128)
            lanes = 128 * core
            stacked[p, 96:864, lanes : lanes + 128] = before.astype(jnp.bfloat16)
            stacked[p, 96:864, 256 + lanes : 384 + lanes] = act
            stacked[p, 96:864, 512 + lanes : 640 + lanes] = after.astype(jnp.bfloat16)

    def product(p, b, matrix):
        rows = stacked[p, 96 * b : 96 * b + 768, :]
        return jnp.dot(rows, matrix[b], preferred_element_type=jnp.float32)

    for p in range(2):
        total = sum(product(p, b, diag) for b in range(TAPS))
        if p == 1:
            total = total + sum(product(0, b, lower) for b in range(TAPS))
        total = total.reshape(8, 96, 256)
        for t in range(4):
            start = 24 * t
            left = total[:, start : start + 8]
            if t > 0:
                share = blend[t - 1][None]
                left = share * total[:, start - 8 : start] + (1.0 - share) * left
            summed[:, 16 * t : 16 * t + 8, :] = left
            summed[:, 16 * t + 8 : 16 * t + 16, :] = total[:, start + 8 : start + 16]
        summed[:, 64:72, :] = total[:, 88:96]
        for t in range(4):
            blocks[p, t] = summed[:, 4 + 16 * t : 20 + 16 * t, :]
    own[...] = blocks[x, z]
    for k in range(1, 4):
        sends[k - 1][...] = blocks[x, z ^ k].astype(jnp.bfloat16)
    for i, k in enumerate((0, 2)):
        kept[i] = blocks[1 - x, z ^ k]
        passed[i] = blocks[1 - x, z ^ k ^ 1].astype(jnp.bfloat16)


def add_body(pos, kept, came, *sums):
    for i in range(2):
        sums[i][...] = (kept[i] + came[i].astype(jnp.float32)).astype(jnp.bfloat16)


def join_body(pos, bias, own, *refs):
    same, far, out = refs[:3], refs[3:5], refs[5]
    x = pos[1]
    near_sum = own[...]
    for part in same:
        near_sum = near_sum + part[...].astype(jnp.float32)
    far_sum = far[0][...].astype(jnp.float32) + far[1][...].astype(jnp.float32)
    low = jnp.where(x == 0, near_sum, far_sum)
    high = jnp.where(x == 0, far_sum, near_sum)
    for f in range(2):
        lanes = slice(128 * f, 128 * f + 128)
        out[f, :, :, 0:128] = (low[..., lanes] + bias[:, 0:128][None]).astype(jnp.bfloat16)
        out[f, :, :, 128:256] = (high[..., lanes] + bias[:, 128:256][None]).astype(jnp.bfloat16)


def exchanged(block, k, j):
    tms = lax.axis_size("tm")
    tiles = lax.axis_size("tile")
    route = [(t * tms + m, (t ^ k) * tms + (m ^ j)) for t in range(tiles) for m in range(tms)]
    return lax.ppermute(block, ("tile", "tm"), route)


def across(block, j):
    route = [(2 * m + c, 2 * (m ^ j) + (1 - c)) for m in range(2) for c in range(2)]
    return lax.ppermute(block, ("tm", "ch"), route)


def resident_plan(latent, norm_gain, norm_shift, kernel, conv_bias, blend_profile):
    bf16, f32 = jnp.bfloat16, jnp.float32
    z, x, c = lax.axis_index("tile"), lax.axis_index("tm"), lax.axis_index("ch")
    pos = jnp.stack([z, x]).astype(jnp.int32)
    block = jax.ShapeDtypeStruct((8, 16, 128), bf16)
    wide = jax.ShapeDtypeStruct((8, 16, 256), bf16)

    def quarter(core, frame_block):
        start = core * 256 + frame_block * 128
        return lax.dynamic_slice_in_dim(kernel, start, 128, axis=4)

    quarters = (quarter(c, x), quarter(1 - c, x), quarter(c, 1 - x), quarter(1 - c, 1 - x))
    latent, quarters = lax.optimization_barrier((latent, quarters))
    same = quarters[0]
    other = across(quarters[1], 0)
    same_far = exchanged(quarters[2], 0, 1)
    other_far = across(quarters[3], 1)
    packed = call(pack_body, [block] * 4)(pos, latent)
    near = [packed[0]] + [exchanged(packed[k], k, 0) for k in (1, 2, 3)]
    same_far, near[2] = lax.optimization_barrier((same_far, near[2]))
    far = [exchanged(part, 0, 1) for part in near]
    matrix = jax.ShapeDtypeStruct((TAPS, 768, 256), bf16)
    diag, lower = call(weights_body, [matrix] * 2)(pos, same, other, same_far, other_far)

    def lanes_of(vector):
        part = lax.dynamic_slice_in_dim(vector, z * 64, 64)
        return jnp.concatenate([part, part])[None]

    acts = call(
        norm_body,
        jax.ShapeDtypeStruct((2, 8, 96, 128), bf16),
        [pltpu.VMEM((2, 4, 8, 16, 128), bf16), pltpu.VMEM((2, 8, 72, 128), f32)],
    )(pos, lanes_of(norm_gain), lanes_of(norm_shift), *near, *far)
    sibling = lax.ppermute(acts, "ch", [(0, 1), (1, 0)])

    offsets = jnp.arange(2 * RIM, dtype=jnp.int32)
    ramps = ramp_weight(blend_profile[:3, None], offsets[None, :], RIM)
    blend = jnp.broadcast_to(ramps[:, :, None], (3, 2 * RIM, 256))
    own, *sends, kept, leaving = call(
        conv_body,
        [jax.ShapeDtypeStruct((8, 16, 256), f32)]
        + [wide] * 3
        + [jax.ShapeDtypeStruct((2, 8, 16, 256), t) for t in (f32, bf16)],
        [
            pltpu.VMEM((2, 960, 768), bf16),
            pltpu.VMEM((8, 72, 256), f32),
            pltpu.VMEM((2, 4, 8, 16, 256), f32),
        ],
    )(pos, acts, sibling, diag, lower, blend)
    came = exchanged(leaving, 1, 0)
    came, sends[0] = lax.optimization_barrier((came, sends[0]))
    sums = call(add_body, [wide] * 2)(pos, kept, came)
    far_sums = [exchanged(sums[1], 2, 1), exchanged(sums[0], 0, 1)]
    near_sums = [exchanged(sends[k - 1], k, 0) for k in (2, 3, 1)]
    return call(join_body, jax.ShapeDtypeStruct(latent.shape, bf16))(
        pos, conv_bias[None], own, *near_sums, *far_sums
    )


def solution(mesh):
    in_specs = (
        P(("grp", "tm"), None, "tile", "ch"),
        P("ch"),
        P("ch"),
        P(None, None, None, ("ch", "tile", "tm"), None),
        P("ch"),
        P(),
    )
    out_specs = P(("grp", "tm"), None, "tile", "ch")

    def on_device(latent, norm_gain, norm_shift, kernel, conv_bias, blend_profile):
        plan = resident_plan if resident_fits(mesh.shape, latent, kernel) else gathered_plan
        return plan(latent, norm_gain, norm_shift, kernel, conv_bias, blend_profile)

    return jax.shard_map(
        on_device, mesh=mesh, in_specs=in_specs, out_specs=out_specs, check_vma=False
    )
```

```python
import functools

import jax
import jax.numpy as jnp
from jax import lax
from jax.experimental import pallas as pl
from jax.experimental.pallas import tpu as pltpu
from jax.sharding import PartitionSpec as P

GROUPS = 32
RIM = 4
TAPS = 3


def ramp_weight(profile, position, margin):
    fraction = (position.astype(jnp.float32) + 0.5) / (2.0 * margin)
    exponent = 1.0 + profile.astype(jnp.float32)
    near_part = jnp.power(1.0 - fraction, exponent)
    far_part = jnp.power(fraction, exponent)
    return near_part / (near_part + far_part)


def with_halo(shard, sides, width):
    for axis, dim in sides:
        size, length = (lax.axis_size(axis), shard.shape[dim])
        up = [(i, (i + 1) % size) for i in range(size - 1)]
        down = [(j, i) for i, j in up]
        last = lax.slice_in_dim(shard, length - width, length, axis=dim)
        leading = lax.slice_in_dim(shard, 0, width, axis=dim)
        before = lax.ppermute(last, axis, up)
        after = lax.ppermute(leading, axis, down)
        shard = jnp.concatenate([before, shard, after], axis=dim)
    return shard


def passed_along(block, axis, distance):
    devices = range(lax.axis_size(axis))
    route = [(i - distance, i) for i in devices if i - distance in devices]
    return lax.ppermute(block, axis, route)


def frame_stats(values, colmask, groups):
    frame_count, row_count, col_count, chan_count = values.shape
    grouped = values.reshape(frame_count, row_count, col_count, groups, chan_count // groups)
    weight = colmask.reshape(1, 1, col_count, 1, 1)
    counted = row_count * (chan_count // groups) * jnp.sum(colmask)
    center = jnp.sum(grouped * weight, axis=(1, 2, 4)) / counted
    spread = (grouped - center[:, None, None, :, None]) * weight
    inverse = lax.rsqrt(jnp.sum(spread * spread, axis=(1, 2, 4)) / counted + 1e-06)
    return (center, inverse)


def activate(values, center, inverse, norm_gain, norm_shift, colmask, timemask, groups):
    frame_count, row_count, col_count, chan_count = values.shape
    grouped = values.reshape(frame_count, row_count, col_count, groups, chan_count // groups)
    normed = (grouped - center[:, None, None, :, None]) * inverse[:, None, None, :, None]
    normed = normed.reshape(values.shape) * norm_gain + norm_shift
    masked = jax.nn.silu(normed) * colmask[None, None, :, None] * timemask[:, None, None, None]
    return masked.astype(jnp.bfloat16)


def conv_taps(padded, kernel_part, frame_count, row_count, col_count):
    in_width = kernel_part.shape[3]
    running = None
    for tap_time in range(3):
        for tap_row in range(3):
            for tap_col in range(3):
                window = padded[
                    tap_time : tap_time + frame_count,
                    tap_row : tap_row + row_count,
                    tap_col : tap_col + col_count,
                ]
                contrib = jnp.dot(
                    window.reshape(-1, in_width),
                    kernel_part[tap_time, tap_row, tap_col],
                    preferred_element_type=jnp.float32,
                )
                running = contrib if running is None else running + contrib
    return running


def gathered_plan(latent, norm_gain, norm_shift, kernel, conv_bias, blend_profile):
    frame_count, row_count, core_cols, chan_half = latent.shape
    out_chans = kernel.shape[4]
    groups = GROUPS // lax.axis_size("ch")
    ncols = core_cols + 2 * RIM
    tile_pos = lax.axis_index("tile")
    tile_count = lax.axis_size("tile")
    window_in = with_halo(latent, (("tile", 2),), RIM)
    cached = passed_along(window_in, "tm", 1)
    frames = jnp.concatenate([cached, window_in], axis=0).astype(jnp.float32)
    column = tile_pos * core_cols - RIM + jnp.arange(ncols, dtype=jnp.int32)
    colmask = ((column >= 0) & (column < tile_count * core_cols)).astype(jnp.float32)
    started = (lax.axis_index("tm") > 0).astype(jnp.float32)
    timemask = jnp.concatenate(
        [jnp.ones((2,), jnp.float32) * started, jnp.ones((frame_count,), jnp.float32)]
    )
    center, inverse = frame_stats(frames, colmask, groups)
    activated = activate(frames, center, inverse, norm_gain, norm_shift, colmask, timemask, groups)
    padded = jnp.pad(activated, ((0, 0), (1, 1), (1, 1), (0, 0)))
    whole_kernel = lax.all_gather(kernel, ("tile", "tm"), axis=3, tiled=True)
    running = conv_taps(padded, whole_kernel, frame_count, row_count, ncols)
    joined = running.reshape(frame_count, row_count, ncols, out_chans)
    summed = lax.psum_scatter(joined, "ch", scatter_dimension=3, tiled=True)
    tile_out = (summed + conv_bias).astype(jnp.bfloat16)
    extended = with_halo(tile_out, (("tile", 2),), RIM)
    own_out = tile_out[:, :, RIM : RIM + core_cols]
    left_nbr = extended[:, :, :RIM]
    right_nbr = extended[:, :, ncols + RIM :]
    own_profile = lax.dynamic_index_in_dim(blend_profile, tile_pos, 0, keepdims=False)
    prev_profile = lax.dynamic_index_in_dim(
        blend_profile, jnp.maximum(tile_pos - 1, 0), 0, keepdims=False
    )
    offsets = jnp.arange(RIM, dtype=jnp.int32)
    left_weight = jnp.where(tile_pos > 0, ramp_weight(prev_profile, offsets + RIM, RIM), 0.0)
    right_weight = jnp.where(tile_pos < tile_count - 1, ramp_weight(own_profile, offsets, RIM), 1.0)
    left_wide = left_weight[None, None, :, None]
    right_wide = right_weight[None, None, :, None]
    own_float = own_out.astype(jnp.float32)
    head_cols = own_float[:, :, :RIM] * (1.0 - left_wide) + left_nbr.astype(jnp.float32) * left_wide
    tail_cols = own_float[:, :, core_cols - RIM :] * right_wide + right_nbr.astype(jnp.float32) * (
        1.0 - right_wide
    )
    middle = own_float[:, :, RIM : core_cols - RIM]
    return jnp.concatenate([head_cols, middle, tail_cols], axis=2).astype(jnp.bfloat16)


VMEM_BYTES = 48 * 1024 * 1024


def resident_fits(mesh, latent, kernel):
    return (
        mesh["tile"] == 4
        and mesh["tm"] == 2
        and mesh["ch"] == 2
        and latent.shape == (2, 8, 16, 256)
        and kernel.shape == (TAPS, TAPS, TAPS, 32, 512)
    )


def call(body, outs, scratch=(), smem_first=True):
    vmem = pl.BlockSpec(memory_space=pltpu.VMEM)
    smem = pl.BlockSpec(memory_space=pltpu.SMEM)

    def run(*args):
        specs = [smem if smem_first and i == 0 else vmem for i in range(len(args))]
        return pl.pallas_call(
            body,
            out_shape=outs,
            in_specs=specs,
            out_specs=jax.tree.map(lambda _: vmem, outs),
            scratch_shapes=list(scratch),
            compiler_params=pltpu.CompilerParams(vmem_limit_bytes=VMEM_BYTES),
            cost_estimate=pl.CostEstimate(flops=1000, bytes_accessed=1000, transcendentals=0),
        )(*args)

    return run


def pack_body(pos, latent, *outs):
    z = pos[0]
    first = latent[0].astype(jnp.float32)
    second = latent[1].astype(jnp.float32)
    for owner in range(4):
        lanes = slice(64 * owner, 64 * owner + 64)
        block = jnp.concatenate([first[..., lanes], second[..., lanes]], axis=-1)
        block = block.astype(jnp.bfloat16)
        for k in range(4):

            @pl.when(z == owner ^ k)
            def _():
                outs[k][...] = block


def group_sum(rows):
    count = rows.shape[0]
    row = lax.broadcasted_iota(jnp.int32, (128, 128), 0)
    lane = lax.broadcasted_iota(jnp.int32, (128, 128), 1)
    same = (row >> 4 == lane >> 4).astype(jnp.bfloat16)
    terms = []
    for _ in range(3):
        term = rows.astype(jnp.bfloat16)
        terms.append(term.astype(jnp.float32))
        rows = rows - term.astype(jnp.float32)
    terms = jnp.concatenate(terms, axis=0).astype(jnp.bfloat16)
    sums = jnp.dot(terms, same, preferred_element_type=jnp.float32)
    return sums[:count] + sums[count : 2 * count] + sums[2 * count :]


def norm_body(pos, gain, shift, *refs):
    blocks, (out, placed, raw) = refs[:8], refs[8:]
    z, x = pos[0], pos[1]
    for k in range(4):
        placed[x, z ^ k] = blocks[k][...]
        placed[1 - x, z ^ k] = blocks[4 + k][...]
    for p in range(2):
        raw[p, :, 0:4, :] = jnp.zeros((8, 4, 128), jnp.float32)
        raw[p, :, 68:72, :] = jnp.zeros((8, 4, 128), jnp.float32)
        for t in range(4):
            raw[p, :, 4 + 16 * t : 20 + 16 * t, :] = placed[p, t].astype(jnp.float32)
    col = lax.broadcasted_iota(jnp.int32, (24, 128), 0)
    present = {0: col >= 4, 3: col < 20}
    count_row = lax.broadcasted_iota(jnp.int32, (8, 128), 0) % 4
    cells = jnp.where((count_row == 0) | (count_row == 3), 20.0, 24.0) * 128.0

    def window(p, t):
        return raw[p, :, 16 * t : 16 * t + 24, :]

    sums = []
    for p in range(2):
        for t in range(4):
            over_rows = jnp.sum(window(p, t), axis=0)
            sums.append(jnp.sum(over_rows, axis=0, keepdims=True))
    center = group_sum(jnp.concatenate(sums, axis=0)) / cells
    sums = []
    for p in range(2):
        for t in range(4):
            at = 4 * p + t
            spread = window(p, t) - center[at : at + 1][None]
            over_rows = jnp.sum(spread * spread, axis=0)
            if t in present:
                over_rows = jnp.where(present[t], over_rows, 0.0)
            sums.append(jnp.sum(over_rows, axis=0, keepdims=True))
    inverse = lax.rsqrt(group_sum(jnp.concatenate(sums, axis=0)) / cells + 1e-06)
    scale = inverse * gain[...]
    offset = shift[...]
    for p in range(2):
        for half in range(2):
            acts = []
            for t in (2 * half, 2 * half + 1):
                at = 4 * p + t
                normed = (window(p, t) - center[at : at + 1][None]) * scale[at : at + 1][None]
                near = 0.5 * (normed + offset[None])
                act = near + near * jnp.tanh(near)
                if t in present:
                    act = jnp.where(present[t][None], act, 0.0)
                acts.append(act)
            joined = jnp.concatenate(acts, axis=1).astype(jnp.bfloat16)
            out[p, :, 48 * half : 48 * half + 48, :] = joined


def weights_body(pos, same, other, same_far, other_far, diag, lower):
    x = pos[1]
    zero = jnp.zeros((32, 128), jnp.bfloat16)
    for b in range(TAPS):
        for e in range(TAPS):
            for core, (near, far) in enumerate(((same, same_far), (other, other_far))):
                for f in range(2):
                    base = e * 256 + core * 128 + f * 64
                    for g in range(2):
                        tap_d, tap_l = f - g + 2, f - g
                        for source, slot in ((near, x), (far, 1 - x)):
                            rows = pl.ds(pl.multiple_of(base + 32 * slot, 32), 32)
                            lanes = slice(128 * g, 128 * g + 128)
                            diag[b, rows, lanes] = source[tap_d, b, e] if tap_d < 3 else zero
                            lower[b, rows, lanes] = source[tap_l, b, e] if tap_l >= 0 else zero


def conv_body(pos, mine, sibling, diag, lower, blend, *refs):
    own, sends, kept, passed, (stacked, summed, blocks) = refs[0], refs[1:4], refs[4], refs[5], refs[6:]
    z, x = pos[0], pos[1]
    col = lax.broadcasted_iota(jnp.int32, (24, 128), 0)
    for p in range(2):
        edge = jnp.zeros((96, 768), jnp.bfloat16)
        stacked[p, 0:96, :] = edge
        stacked[p, 864:960, :] = edge
        for core, source in enumerate((mine, sibling)):
            act = source[p].reshape(768, 128)
            wide = act.astype(jnp.float32)
            before = pltpu.roll(wide, 1, 0).reshape(32, 24, 128)
            before = jnp.where((col > 0)[None], before, 0.0).reshape(768, 128)
            after = pltpu.roll(wide, 767, 0).reshape(32, 24, 128)
            after = jnp.where((col < 23)[None], after, 0.0).reshape(768, 128)
            lanes = 128 * core
            stacked[p, 96:864, lanes : lanes + 128] = before.astype(jnp.bfloat16)
            stacked[p, 96:864, 256 + lanes : 384 + lanes] = act
            stacked[p, 96:864, 512 + lanes : 640 + lanes] = after.astype(jnp.bfloat16)

    def product(p, b, matrix):
        rows = stacked[p, 96 * b : 96 * b + 768, :]
        return jnp.dot(rows, matrix[b], preferred_element_type=jnp.float32)

    for p in range(2):
        total = sum(product(p, b, diag) for b in range(TAPS))
        if p == 1:
            total = total + sum(product(0, b, lower) for b in range(TAPS))
        total = total.reshape(8, 96, 256)
        for t in range(4):
            start = 24 * t
            left = total[:, start : start + 8]
            if t > 0:
                share = blend[t - 1][None]
                left = share * total[:, start - 8 : start] + (1.0 - share) * left
            summed[:, 16 * t : 16 * t + 8, :] = left
            summed[:, 16 * t + 8 : 16 * t + 16, :] = total[:, start + 8 : start + 16]
        summed[:, 64:72, :] = total[:, 88:96]
        for t in range(4):
            blocks[p, t] = summed[:, 4 + 16 * t : 20 + 16 * t, :]
    own[...] = blocks[x, z]
    for k in range(1, 4):
        sends[k - 1][...] = blocks[x, z ^ k].astype(jnp.bfloat16)
    for i, k in enumerate((0, 2)):
        kept[i] = blocks[1 - x, z ^ k]
        passed[i] = blocks[1 - x, z ^ k ^ 1].astype(jnp.bfloat16)


def add_body(pos, kept, came, *sums):
    for i in range(2):
        sums[i][...] = (kept[i] + came[i].astype(jnp.float32)).astype(jnp.bfloat16)


def join_body(pos, bias, own, *refs):
    same, far, out = refs[:3], refs[3:5], refs[5]
    x = pos[1]
    near_sum = own[...]
    for part in same:
        near_sum = near_sum + part[...].astype(jnp.float32)
    far_sum = far[0][...].astype(jnp.float32) + far[1][...].astype(jnp.float32)
    low = jnp.where(x == 0, near_sum, far_sum)
    high = jnp.where(x == 0, far_sum, near_sum)
    for f in range(2):
        lanes = slice(128 * f, 128 * f + 128)
        out[f, :, :, 0:128] = (low[..., lanes] + bias[:, 0:128][None]).astype(jnp.bfloat16)
        out[f, :, :, 128:256] = (high[..., lanes] + bias[:, 128:256][None]).astype(jnp.bfloat16)


def exchanged(block, k, j):
    tms = lax.axis_size("tm")
    tiles = lax.axis_size("tile")
    route = [(t * tms + m, (t ^ k) * tms + (m ^ j)) for t in range(tiles) for m in range(tms)]
    return lax.ppermute(block, ("tile", "tm"), route)


def across(block, j):
    route = [(2 * m + c, 2 * (m ^ j) + (1 - c)) for m in range(2) for c in range(2)]
    return lax.ppermute(block, ("tm", "ch"), route)


def resident_plan(latent, norm_gain, norm_shift, kernel, conv_bias, blend_profile):
    bf16, f32 = jnp.bfloat16, jnp.float32
    z, x, c = lax.axis_index("tile"), lax.axis_index("tm"), lax.axis_index("ch")
    pos = jnp.stack([z, x]).astype(jnp.int32)
    block = jax.ShapeDtypeStruct((8, 16, 128), bf16)
    wide = jax.ShapeDtypeStruct((8, 16, 256), bf16)

    def quarter(core, frame_block):
        start = core * 256 + frame_block * 128
        return lax.dynamic_slice_in_dim(kernel, start, 128, axis=4)

    quarters = (quarter(c, x), quarter(1 - c, x), quarter(c, 1 - x), quarter(1 - c, 1 - x))
    latent, quarters = lax.optimization_barrier((latent, quarters))
    same = quarters[0]
    other = across(quarters[1], 0)
    same_far = exchanged(quarters[2], 0, 1)
    other_far = across(quarters[3], 1)
    packed = call(pack_body, [block] * 4)(pos, latent)
    near = [packed[0]] + [exchanged(packed[k], k, 0) for k in (1, 2, 3)]
    other_far, near[3] = lax.optimization_barrier((other_far, near[3]))
    far = [exchanged(part, 0, 1) for part in near]
    matrix = jax.ShapeDtypeStruct((TAPS, 768, 256), bf16)
    diag, lower = call(weights_body, [matrix] * 2)(pos, same, other, same_far, other_far)

    def lanes_of(vector):
        part = lax.dynamic_slice_in_dim(vector, z * 64, 64)
        return jnp.concatenate([part, part])[None]

    acts = call(
        norm_body,
        jax.ShapeDtypeStruct((2, 8, 96, 128), bf16),
        [pltpu.VMEM((2, 4, 8, 16, 128), bf16), pltpu.VMEM((2, 8, 72, 128), f32)],
    )(pos, lanes_of(norm_gain), lanes_of(norm_shift), *near, *far)
    sibling = lax.ppermute(acts, "ch", [(0, 1), (1, 0)])

    offsets = jnp.arange(2 * RIM, dtype=jnp.int32)
    ramps = ramp_weight(blend_profile[:3, None], offsets[None, :], RIM)
    blend = jnp.broadcast_to(ramps[:, :, None], (3, 2 * RIM, 256))
    own, *sends, kept, leaving = call(
        conv_body,
        [jax.ShapeDtypeStruct((8, 16, 256), f32)]
        + [wide] * 3
        + [jax.ShapeDtypeStruct((2, 8, 16, 256), t) for t in (f32, bf16)],
        [
            pltpu.VMEM((2, 960, 768), bf16),
            pltpu.VMEM((8, 72, 256), f32),
            pltpu.VMEM((2, 4, 8, 16, 256), f32),
        ],
    )(pos, acts, sibling, diag, lower, blend)
    came = exchanged(leaving, 1, 0)
    came, sends[0] = lax.optimization_barrier((came, sends[0]))
    sums = call(add_body, [wide] * 2)(pos, kept, came)
    far_sums = [exchanged(sums[1], 2, 1), exchanged(sums[0], 0, 1)]
    near_sums = [exchanged(sends[k - 1], k, 0) for k in (2, 3, 1)]
    return call(join_body, jax.ShapeDtypeStruct(latent.shape, bf16))(
        pos, conv_bias[None], own, *near_sums, *far_sums
    )


def solution(mesh):
    in_specs = (
        P(("grp", "tm"), None, "tile", "ch"),
        P("ch"),
        P("ch"),
        P(None, None, None, ("ch", "tile", "tm"), None),
        P("ch"),
        P(),
    )
    out_specs = P(("grp", "tm"), None, "tile", "ch")

    def on_device(latent, norm_gain, norm_shift, kernel, conv_bias, blend_profile):
        plan = resident_plan if resident_fits(mesh.shape, latent, kernel) else gathered_plan
        return plan(latent, norm_gain, norm_shift, kernel, conv_bias, blend_profile)

    return jax.shard_map(
        on_device, mesh=mesh, in_specs=in_specs, out_specs=out_specs, check_vma=False
    )
```

```python
import functools

import jax
import jax.numpy as jnp
from jax import lax
from jax.experimental import pallas as pl
from jax.experimental.pallas import tpu as pltpu
from jax.sharding import PartitionSpec as P

GROUPS = 32
RIM = 4
TAPS = 3


def ramp_weight(profile, position, margin):
    fraction = (position.astype(jnp.float32) + 0.5) / (2.0 * margin)
    exponent = 1.0 + profile.astype(jnp.float32)
    near_part = jnp.power(1.0 - fraction, exponent)
    far_part = jnp.power(fraction, exponent)
    return near_part / (near_part + far_part)


def with_halo(shard, sides, width):
    for axis, dim in sides:
        size, length = (lax.axis_size(axis), shard.shape[dim])
        up = [(i, (i + 1) % size) for i in range(size - 1)]
        down = [(j, i) for i, j in up]
        last = lax.slice_in_dim(shard, length - width, length, axis=dim)
        leading = lax.slice_in_dim(shard, 0, width, axis=dim)
        before = lax.ppermute(last, axis, up)
        after = lax.ppermute(leading, axis, down)
        shard = jnp.concatenate([before, shard, after], axis=dim)
    return shard


def passed_along(block, axis, distance):
    devices = range(lax.axis_size(axis))
    route = [(i - distance, i) for i in devices if i - distance in devices]
    return lax.ppermute(block, axis, route)


def frame_stats(values, colmask, groups):
    frame_count, row_count, col_count, chan_count = values.shape
    grouped = values.reshape(frame_count, row_count, col_count, groups, chan_count // groups)
    weight = colmask.reshape(1, 1, col_count, 1, 1)
    counted = row_count * (chan_count // groups) * jnp.sum(colmask)
    center = jnp.sum(grouped * weight, axis=(1, 2, 4)) / counted
    spread = (grouped - center[:, None, None, :, None]) * weight
    inverse = lax.rsqrt(jnp.sum(spread * spread, axis=(1, 2, 4)) / counted + 1e-06)
    return (center, inverse)


def activate(values, center, inverse, norm_gain, norm_shift, colmask, timemask, groups):
    frame_count, row_count, col_count, chan_count = values.shape
    grouped = values.reshape(frame_count, row_count, col_count, groups, chan_count // groups)
    normed = (grouped - center[:, None, None, :, None]) * inverse[:, None, None, :, None]
    normed = normed.reshape(values.shape) * norm_gain + norm_shift
    masked = jax.nn.silu(normed) * colmask[None, None, :, None] * timemask[:, None, None, None]
    return masked.astype(jnp.bfloat16)


def conv_taps(padded, kernel_part, frame_count, row_count, col_count):
    in_width = kernel_part.shape[3]
    running = None
    for tap_time in range(3):
        for tap_row in range(3):
            for tap_col in range(3):
                window = padded[
                    tap_time : tap_time + frame_count,
                    tap_row : tap_row + row_count,
                    tap_col : tap_col + col_count,
                ]
                contrib = jnp.dot(
                    window.reshape(-1, in_width),
                    kernel_part[tap_time, tap_row, tap_col],
                    preferred_element_type=jnp.float32,
                )
                running = contrib if running is None else running + contrib
    return running


def gathered_plan(latent, norm_gain, norm_shift, kernel, conv_bias, blend_profile):
    frame_count, row_count, core_cols, chan_half = latent.shape
    out_chans = kernel.shape[4]
    groups = GROUPS // lax.axis_size("ch")
    ncols = core_cols + 2 * RIM
    tile_pos = lax.axis_index("tile")
    tile_count = lax.axis_size("tile")
    window_in = with_halo(latent, (("tile", 2),), RIM)
    cached = passed_along(window_in, "tm", 1)
    frames = jnp.concatenate([cached, window_in], axis=0).astype(jnp.float32)
    column = tile_pos * core_cols - RIM + jnp.arange(ncols, dtype=jnp.int32)
    colmask = ((column >= 0) & (column < tile_count * core_cols)).astype(jnp.float32)
    started = (lax.axis_index("tm") > 0).astype(jnp.float32)
    timemask = jnp.concatenate(
        [jnp.ones((2,), jnp.float32) * started, jnp.ones((frame_count,), jnp.float32)]
    )
    center, inverse = frame_stats(frames, colmask, groups)
    activated = activate(frames, center, inverse, norm_gain, norm_shift, colmask, timemask, groups)
    padded = jnp.pad(activated, ((0, 0), (1, 1), (1, 1), (0, 0)))
    whole_kernel = lax.all_gather(kernel, ("tile", "tm"), axis=3, tiled=True)
    running = conv_taps(padded, whole_kernel, frame_count, row_count, ncols)
    joined = running.reshape(frame_count, row_count, ncols, out_chans)
    summed = lax.psum_scatter(joined, "ch", scatter_dimension=3, tiled=True)
    tile_out = (summed + conv_bias).astype(jnp.bfloat16)
    extended = with_halo(tile_out, (("tile", 2),), RIM)
    own_out = tile_out[:, :, RIM : RIM + core_cols]
    left_nbr = extended[:, :, :RIM]
    right_nbr = extended[:, :, ncols + RIM :]
    own_profile = lax.dynamic_index_in_dim(blend_profile, tile_pos, 0, keepdims=False)
    prev_profile = lax.dynamic_index_in_dim(
        blend_profile, jnp.maximum(tile_pos - 1, 0), 0, keepdims=False
    )
    offsets = jnp.arange(RIM, dtype=jnp.int32)
    left_weight = jnp.where(tile_pos > 0, ramp_weight(prev_profile, offsets + RIM, RIM), 0.0)
    right_weight = jnp.where(tile_pos < tile_count - 1, ramp_weight(own_profile, offsets, RIM), 1.0)
    left_wide = left_weight[None, None, :, None]
    right_wide = right_weight[None, None, :, None]
    own_float = own_out.astype(jnp.float32)
    head_cols = own_float[:, :, :RIM] * (1.0 - left_wide) + left_nbr.astype(jnp.float32) * left_wide
    tail_cols = own_float[:, :, core_cols - RIM :] * right_wide + right_nbr.astype(jnp.float32) * (
        1.0 - right_wide
    )
    middle = own_float[:, :, RIM : core_cols - RIM]
    return jnp.concatenate([head_cols, middle, tail_cols], axis=2).astype(jnp.bfloat16)


VMEM_BYTES = 48 * 1024 * 1024


def resident_fits(mesh, latent, kernel):
    return (
        mesh["tile"] == 4
        and mesh["tm"] == 2
        and mesh["ch"] == 2
        and latent.shape == (2, 8, 16, 256)
        and kernel.shape == (TAPS, TAPS, TAPS, 32, 512)
    )


def call(body, outs, scratch=(), smem_first=True):
    vmem = pl.BlockSpec(memory_space=pltpu.VMEM)
    smem = pl.BlockSpec(memory_space=pltpu.SMEM)

    def run(*args):
        specs = [smem if smem_first and i == 0 else vmem for i in range(len(args))]
        return pl.pallas_call(
            body,
            out_shape=outs,
            in_specs=specs,
            out_specs=jax.tree.map(lambda _: vmem, outs),
            scratch_shapes=list(scratch),
            compiler_params=pltpu.CompilerParams(vmem_limit_bytes=VMEM_BYTES),
            cost_estimate=pl.CostEstimate(flops=1000, bytes_accessed=1000, transcendentals=0),
        )(*args)

    return run


def pack_body(pos, latent, *outs):
    z = pos[0]
    first = latent[0].astype(jnp.float32)
    second = latent[1].astype(jnp.float32)
    for owner in range(4):
        lanes = slice(64 * owner, 64 * owner + 64)
        block = jnp.concatenate([first[..., lanes], second[..., lanes]], axis=-1)
        block = block.astype(jnp.bfloat16)
        for k in range(4):

            @pl.when(z == owner ^ k)
            def _():
                outs[k][...] = block


def group_sum(rows):
    count = rows.shape[0]
    row = lax.broadcasted_iota(jnp.int32, (128, 128), 0)
    lane = lax.broadcasted_iota(jnp.int32, (128, 128), 1)
    same = (row >> 4 == lane >> 4).astype(jnp.bfloat16)
    terms = []
    for _ in range(3):
        term = rows.astype(jnp.bfloat16)
        terms.append(term.astype(jnp.float32))
        rows = rows - term.astype(jnp.float32)
    terms = jnp.concatenate(terms, axis=0).astype(jnp.bfloat16)
    sums = jnp.dot(terms, same, preferred_element_type=jnp.float32)
    return sums[:count] + sums[count : 2 * count] + sums[2 * count :]


def norm_body(pos, gain, shift, *refs):
    blocks, (out, placed, raw) = refs[:8], refs[8:]
    z, x = pos[0], pos[1]
    for k in range(4):
        placed[x, z ^ k] = blocks[k][...]
        placed[1 - x, z ^ k] = blocks[4 + k][...]
    for p in range(2):
        raw[p, :, 0:4, :] = jnp.zeros((8, 4, 128), jnp.float32)
        raw[p, :, 68:72, :] = jnp.zeros((8, 4, 128), jnp.float32)
        for t in range(4):
            raw[p, :, 4 + 16 * t : 20 + 16 * t, :] = placed[p, t].astype(jnp.float32)
    col = lax.broadcasted_iota(jnp.int32, (24, 128), 0)
    present = {0: col >= 4, 3: col < 20}
    count_row = lax.broadcasted_iota(jnp.int32, (8, 128), 0) % 4
    cells = jnp.where((count_row == 0) | (count_row == 3), 20.0, 24.0) * 128.0

    def window(p, t):
        return raw[p, :, 16 * t : 16 * t + 24, :]

    sums = []
    for p in range(2):
        for t in range(4):
            over_rows = jnp.sum(window(p, t), axis=0)
            sums.append(jnp.sum(over_rows, axis=0, keepdims=True))
    center = group_sum(jnp.concatenate(sums, axis=0)) / cells
    sums = []
    for p in range(2):
        for t in range(4):
            at = 4 * p + t
            spread = window(p, t) - center[at : at + 1][None]
            over_rows = jnp.sum(spread * spread, axis=0)
            if t in present:
                over_rows = jnp.where(present[t], over_rows, 0.0)
            sums.append(jnp.sum(over_rows, axis=0, keepdims=True))
    inverse = lax.rsqrt(group_sum(jnp.concatenate(sums, axis=0)) / cells + 1e-06)
    scale = inverse * gain[...]
    offset = shift[...]
    for p in range(2):
        for half in range(2):
            acts = []
            for t in (2 * half, 2 * half + 1):
                at = 4 * p + t
                normed = (window(p, t) - center[at : at + 1][None]) * scale[at : at + 1][None]
                near = 0.5 * (normed + offset[None])
                act = near + near * jnp.tanh(near)
                if t in present:
                    act = jnp.where(present[t][None], act, 0.0)
                acts.append(act)
            joined = jnp.concatenate(acts, axis=1).astype(jnp.bfloat16)
            out[p, :, 48 * half : 48 * half + 48, :] = joined


def weights_body(pos, same, other, same_far, other_far, diag, lower):
    x = pos[1]
    zero = jnp.zeros((32, 128), jnp.bfloat16)
    for b in range(TAPS):
        for e in range(TAPS):
            for core, (near, far) in enumerate(((same, same_far), (other, other_far))):
                for f in range(2):
                    base = e * 256 + core * 128 + f * 64
                    for g in range(2):
                        tap_d, tap_l = f - g + 2, f - g
                        for source, slot in ((near, x), (far, 1 - x)):
                            rows = pl.ds(pl.multiple_of(base + 32 * slot, 32), 32)
                            lanes = slice(128 * g, 128 * g + 128)
                            diag[b, rows, lanes] = source[tap_d, b, e] if tap_d < 3 else zero
                            lower[b, rows, lanes] = source[tap_l, b, e] if tap_l >= 0 else zero


def conv_body(pos, mine, sibling, diag, lower, blend, *refs):
    own, sends, kept, passed, (stacked, summed, blocks) = refs[0], refs[1:4], refs[4], refs[5], refs[6:]
    z, x = pos[0], pos[1]
    col = lax.broadcasted_iota(jnp.int32, (24, 128), 0)
    for p in range(2):
        edge = jnp.zeros((96, 768), jnp.bfloat16)
        stacked[p, 0:96, :] = edge
        stacked[p, 864:960, :] = edge
        for core, source in enumerate((mine, sibling)):
            act = source[p].reshape(768, 128)
            wide = act.astype(jnp.float32)
            before = pltpu.roll(wide, 1, 0).reshape(32, 24, 128)
            before = jnp.where((col > 0)[None], before, 0.0).reshape(768, 128)
            after = pltpu.roll(wide, 767, 0).reshape(32, 24, 128)
            after = jnp.where((col < 23)[None], after, 0.0).reshape(768, 128)
            lanes = 128 * core
            stacked[p, 96:864, lanes : lanes + 128] = before.astype(jnp.bfloat16)
            stacked[p, 96:864, 256 + lanes : 384 + lanes] = act
            stacked[p, 96:864, 512 + lanes : 640 + lanes] = after.astype(jnp.bfloat16)

    def product(p, b, matrix):
        rows = stacked[p, 96 * b : 96 * b + 768, :]
        return jnp.dot(rows, matrix[b], preferred_element_type=jnp.float32)

    for p in range(2):
        total = sum(product(p, b, diag) for b in range(TAPS))
        if p == 1:
            total = total + sum(product(0, b, lower) for b in range(TAPS))
        total = total.reshape(8, 96, 256)
        for t in range(4):
            start = 24 * t
            left = total[:, start : start + 8]
            if t > 0:
                share = blend[t - 1][None]
                left = share * total[:, start - 8 : start] + (1.0 - share) * left
            summed[:, 16 * t : 16 * t + 8, :] = left
            summed[:, 16 * t + 8 : 16 * t + 16, :] = total[:, start + 8 : start + 16]
        summed[:, 64:72, :] = total[:, 88:96]
        for t in range(4):
            blocks[p, t] = summed[:, 4 + 16 * t : 20 + 16 * t, :]
    own[...] = blocks[x, z]
    for k in range(1, 4):
        sends[k - 1][...] = blocks[x, z ^ k].astype(jnp.bfloat16)
    for i, k in enumerate((0, 2)):
        kept[i] = blocks[1 - x, z ^ k]
        passed[i] = blocks[1 - x, z ^ k ^ 1].astype(jnp.bfloat16)


def add_body(pos, kept, came, *sums):
    for i in range(2):
        sums[i][...] = (kept[i] + came[i].astype(jnp.float32)).astype(jnp.bfloat16)


def join_body(pos, bias, own, *refs):
    same, far, out = refs[:3], refs[3:5], refs[5]
    x = pos[1]
    near_sum = own[...]
    for part in same:
        near_sum = near_sum + part[...].astype(jnp.float32)
    far_sum = far[0][...].astype(jnp.float32) + far[1][...].astype(jnp.float32)
    low = jnp.where(x == 0, near_sum, far_sum)
    high = jnp.where(x == 0, far_sum, near_sum)
    for f in range(2):
        lanes = slice(128 * f, 128 * f + 128)
        out[f, :, :, 0:128] = (low[..., lanes] + bias[:, 0:128][None]).astype(jnp.bfloat16)
        out[f, :, :, 128:256] = (high[..., lanes] + bias[:, 128:256][None]).astype(jnp.bfloat16)


def exchanged(block, k, j):
    tms = lax.axis_size("tm")
    tiles = lax.axis_size("tile")
    route = [(t * tms + m, (t ^ k) * tms + (m ^ j)) for t in range(tiles) for m in range(tms)]
    return lax.ppermute(block, ("tile", "tm"), route)


def across(block, j):
    route = [(2 * m + c, 2 * (m ^ j) + (1 - c)) for m in range(2) for c in range(2)]
    return lax.ppermute(block, ("tm", "ch"), route)


def resident_plan(latent, norm_gain, norm_shift, kernel, conv_bias, blend_profile):
    bf16, f32 = jnp.bfloat16, jnp.float32
    z, x, c = lax.axis_index("tile"), lax.axis_index("tm"), lax.axis_index("ch")
    pos = jnp.stack([z, x]).astype(jnp.int32)
    block = jax.ShapeDtypeStruct((8, 16, 128), bf16)
    wide = jax.ShapeDtypeStruct((8, 16, 256), bf16)

    def quarter(core, frame_block):
        start = core * 256 + frame_block * 128
        return lax.dynamic_slice_in_dim(kernel, start, 128, axis=4)

    quarters = (quarter(c, x), quarter(1 - c, x), quarter(c, 1 - x), quarter(1 - c, 1 - x))
    latent, quarters = lax.optimization_barrier((latent, quarters))
    same = quarters[0]
    other = across(quarters[1], 0)
    same_far = exchanged(quarters[2], 0, 1)
    other_far = across(quarters[3], 1)
    packed = call(pack_body, [block] * 4)(pos, latent)
    near = [packed[0]] + [exchanged(packed[k], k, 0) for k in (1, 2, 3)]
    other_far, near[3] = lax.optimization_barrier((other_far, near[3]))
    far = [exchanged(part, 0, 1) for part in near]
    matrix = jax.ShapeDtypeStruct((TAPS, 768, 256), bf16)
    diag, lower = call(weights_body, [matrix] * 2)(pos, same, other, same_far, other_far)

    def lanes_of(vector):
        part = lax.dynamic_slice_in_dim(vector, z * 64, 64)
        return jnp.concatenate([part, part])[None]

    acts = call(
        norm_body,
        jax.ShapeDtypeStruct((2, 8, 96, 128), bf16),
        [pltpu.VMEM((2, 4, 8, 16, 128), bf16), pltpu.VMEM((2, 8, 72, 128), f32)],
    )(pos, lanes_of(norm_gain), lanes_of(norm_shift), *near, *far)
    sibling = lax.ppermute(acts, "ch", [(0, 1), (1, 0)])

    offsets = jnp.arange(2 * RIM, dtype=jnp.int32)
    ramps = ramp_weight(blend_profile[:3, None], offsets[None, :], RIM)
    blend = jnp.broadcast_to(ramps[:, :, None], (3, 2 * RIM, 256))
    own, *sends, kept, leaving = call(
        conv_body,
        [jax.ShapeDtypeStruct((8, 16, 256), f32)]
        + [wide] * 3
        + [jax.ShapeDtypeStruct((2, 8, 16, 256), t) for t in (f32, bf16)],
        [
            pltpu.VMEM((2, 960, 768), bf16),
            pltpu.VMEM((8, 72, 256), f32),
            pltpu.VMEM((2, 4, 8, 16, 256), f32),
        ],
    )(pos, acts, sibling, diag, lower, blend)
    came = exchanged(leaving, 1, 0)
    came, sends[0] = lax.optimization_barrier((came, sends[0]))
    sums = call(add_body, [wide] * 2)(pos, kept, came)
    far_sums = [exchanged(sums[1], 2, 1), exchanged(sums[0], 0, 1)]
    near_sums = [exchanged(sends[k - 1], k, 0) for k in (3, 2, 1)]
    return call(join_body, jax.ShapeDtypeStruct(latent.shape, bf16))(
        pos, conv_bias[None], own, *near_sums, *far_sums
    )


def solution(mesh):
    in_specs = (
        P(("grp", "tm"), None, "tile", "ch"),
        P("ch"),
        P("ch"),
        P(None, None, None, ("ch", "tile", "tm"), None),
        P("ch"),
        P(),
    )
    out_specs = P(("grp", "tm"), None, "tile", "ch")

    def on_device(latent, norm_gain, norm_shift, kernel, conv_bias, blend_profile):
        plan = resident_plan if resident_fits(mesh.shape, latent, kernel) else gathered_plan
        return plan(latent, norm_gain, norm_shift, kernel, conv_bias, blend_profile)

    return jax.shard_map(
        on_device, mesh=mesh, in_specs=in_specs, out_specs=out_specs, check_vma=False
    )
```

```python
import functools

import jax
import jax.numpy as jnp
from jax import lax
from jax.experimental import pallas as pl
from jax.experimental.pallas import tpu as pltpu
from jax.sharding import PartitionSpec as P

GROUPS = 32
RIM = 4
TAPS = 3


def ramp_weight(profile, position, margin):
    fraction = (position.astype(jnp.float32) + 0.5) / (2.0 * margin)
    exponent = 1.0 + profile.astype(jnp.float32)
    near_part = jnp.power(1.0 - fraction, exponent)
    far_part = jnp.power(fraction, exponent)
    return near_part / (near_part + far_part)


def with_halo(shard, sides, width):
    for axis, dim in sides:
        size, length = (lax.axis_size(axis), shard.shape[dim])
        up = [(i, (i + 1) % size) for i in range(size - 1)]
        down = [(j, i) for i, j in up]
        last = lax.slice_in_dim(shard, length - width, length, axis=dim)
        leading = lax.slice_in_dim(shard, 0, width, axis=dim)
        before = lax.ppermute(last, axis, up)
        after = lax.ppermute(leading, axis, down)
        shard = jnp.concatenate([before, shard, after], axis=dim)
    return shard


def passed_along(block, axis, distance):
    devices = range(lax.axis_size(axis))
    route = [(i - distance, i) for i in devices if i - distance in devices]
    return lax.ppermute(block, axis, route)


def frame_stats(values, colmask, groups):
    frame_count, row_count, col_count, chan_count = values.shape
    grouped = values.reshape(frame_count, row_count, col_count, groups, chan_count // groups)
    weight = colmask.reshape(1, 1, col_count, 1, 1)
    counted = row_count * (chan_count // groups) * jnp.sum(colmask)
    center = jnp.sum(grouped * weight, axis=(1, 2, 4)) / counted
    spread = (grouped - center[:, None, None, :, None]) * weight
    inverse = lax.rsqrt(jnp.sum(spread * spread, axis=(1, 2, 4)) / counted + 1e-06)
    return (center, inverse)


def activate(values, center, inverse, norm_gain, norm_shift, colmask, timemask, groups):
    frame_count, row_count, col_count, chan_count = values.shape
    grouped = values.reshape(frame_count, row_count, col_count, groups, chan_count // groups)
    normed = (grouped - center[:, None, None, :, None]) * inverse[:, None, None, :, None]
    normed = normed.reshape(values.shape) * norm_gain + norm_shift
    masked = jax.nn.silu(normed) * colmask[None, None, :, None] * timemask[:, None, None, None]
    return masked.astype(jnp.bfloat16)


def conv_taps(padded, kernel_part, frame_count, row_count, col_count):
    in_width = kernel_part.shape[3]
    running = None
    for tap_time in range(3):
        for tap_row in range(3):
            for tap_col in range(3):
                window = padded[
                    tap_time : tap_time + frame_count,
                    tap_row : tap_row + row_count,
                    tap_col : tap_col + col_count,
                ]
                contrib = jnp.dot(
                    window.reshape(-1, in_width),
                    kernel_part[tap_time, tap_row, tap_col],
                    preferred_element_type=jnp.float32,
                )
                running = contrib if running is None else running + contrib
    return running


def gathered_plan(latent, norm_gain, norm_shift, kernel, conv_bias, blend_profile):
    frame_count, row_count, core_cols, chan_half = latent.shape
    out_chans = kernel.shape[4]
    groups = GROUPS // lax.axis_size("ch")
    ncols = core_cols + 2 * RIM
    tile_pos = lax.axis_index("tile")
    tile_count = lax.axis_size("tile")
    window_in = with_halo(latent, (("tile", 2),), RIM)
    cached = passed_along(window_in, "tm", 1)
    frames = jnp.concatenate([cached, window_in], axis=0).astype(jnp.float32)
    column = tile_pos * core_cols - RIM + jnp.arange(ncols, dtype=jnp.int32)
    colmask = ((column >= 0) & (column < tile_count * core_cols)).astype(jnp.float32)
    started = (lax.axis_index("tm") > 0).astype(jnp.float32)
    timemask = jnp.concatenate(
        [jnp.ones((2,), jnp.float32) * started, jnp.ones((frame_count,), jnp.float32)]
    )
    center, inverse = frame_stats(frames, colmask, groups)
    activated = activate(frames, center, inverse, norm_gain, norm_shift, colmask, timemask, groups)
    padded = jnp.pad(activated, ((0, 0), (1, 1), (1, 1), (0, 0)))
    whole_kernel = lax.all_gather(kernel, ("tile", "tm"), axis=3, tiled=True)
    running = conv_taps(padded, whole_kernel, frame_count, row_count, ncols)
    joined = running.reshape(frame_count, row_count, ncols, out_chans)
    summed = lax.psum_scatter(joined, "ch", scatter_dimension=3, tiled=True)
    tile_out = (summed + conv_bias).astype(jnp.bfloat16)
    extended = with_halo(tile_out, (("tile", 2),), RIM)
    own_out = tile_out[:, :, RIM : RIM + core_cols]
    left_nbr = extended[:, :, :RIM]
    right_nbr = extended[:, :, ncols + RIM :]
    own_profile = lax.dynamic_index_in_dim(blend_profile, tile_pos, 0, keepdims=False)
    prev_profile = lax.dynamic_index_in_dim(
        blend_profile, jnp.maximum(tile_pos - 1, 0), 0, keepdims=False
    )
    offsets = jnp.arange(RIM, dtype=jnp.int32)
    left_weight = jnp.where(tile_pos > 0, ramp_weight(prev_profile, offsets + RIM, RIM), 0.0)
    right_weight = jnp.where(tile_pos < tile_count - 1, ramp_weight(own_profile, offsets, RIM), 1.0)
    left_wide = left_weight[None, None, :, None]
    right_wide = right_weight[None, None, :, None]
    own_float = own_out.astype(jnp.float32)
    head_cols = own_float[:, :, :RIM] * (1.0 - left_wide) + left_nbr.astype(jnp.float32) * left_wide
    tail_cols = own_float[:, :, core_cols - RIM :] * right_wide + right_nbr.astype(jnp.float32) * (
        1.0 - right_wide
    )
    middle = own_float[:, :, RIM : core_cols - RIM]
    return jnp.concatenate([head_cols, middle, tail_cols], axis=2).astype(jnp.bfloat16)


VMEM_BYTES = 48 * 1024 * 1024


def resident_fits(mesh, latent, kernel):
    return (
        mesh["tile"] == 4
        and mesh["tm"] == 2
        and mesh["ch"] == 2
        and latent.shape == (2, 8, 16, 256)
        and kernel.shape == (TAPS, TAPS, TAPS, 32, 512)
    )


def call(body, outs, scratch=(), smem_first=True):
    vmem = pl.BlockSpec(memory_space=pltpu.VMEM)
    smem = pl.BlockSpec(memory_space=pltpu.SMEM)

    def run(*args):
        specs = [smem if smem_first and i == 0 else vmem for i in range(len(args))]
        return pl.pallas_call(
            body,
            out_shape=outs,
            in_specs=specs,
            out_specs=jax.tree.map(lambda _: vmem, outs),
            scratch_shapes=list(scratch),
            compiler_params=pltpu.CompilerParams(vmem_limit_bytes=VMEM_BYTES),
            cost_estimate=pl.CostEstimate(flops=1000, bytes_accessed=1000, transcendentals=0),
        )(*args)

    return run


def pack_body(pos, latent, *outs):
    z = pos[0]
    first = latent[0].astype(jnp.float32)
    second = latent[1].astype(jnp.float32)
    for owner in range(4):
        lanes = slice(64 * owner, 64 * owner + 64)
        block = jnp.concatenate([first[..., lanes], second[..., lanes]], axis=-1)
        block = block.astype(jnp.bfloat16)
        for k in range(4):

            @pl.when(z == owner ^ k)
            def _():
                outs[k][...] = block


def group_sum(rows):
    count = rows.shape[0]
    row = lax.broadcasted_iota(jnp.int32, (128, 128), 0)
    lane = lax.broadcasted_iota(jnp.int32, (128, 128), 1)
    same = (row >> 4 == lane >> 4).astype(jnp.bfloat16)
    terms = []
    for _ in range(3):
        term = rows.astype(jnp.bfloat16)
        terms.append(term.astype(jnp.float32))
        rows = rows - term.astype(jnp.float32)
    terms = jnp.concatenate(terms, axis=0).astype(jnp.bfloat16)
    sums = jnp.dot(terms, same, preferred_element_type=jnp.float32)
    return sums[:count] + sums[count : 2 * count] + sums[2 * count :]


def norm_body(pos, gain, shift, *refs):
    blocks, (out, placed, raw) = refs[:8], refs[8:]
    z, x = pos[0], pos[1]
    for k in range(4):
        placed[x, z ^ k] = blocks[k][...]
        placed[1 - x, z ^ k] = blocks[4 + k][...]
    for p in range(2):
        raw[p, :, 0:4, :] = jnp.zeros((8, 4, 128), jnp.float32)
        raw[p, :, 68:72, :] = jnp.zeros((8, 4, 128), jnp.float32)
        for t in range(4):
            raw[p, :, 4 + 16 * t : 20 + 16 * t, :] = placed[p, t].astype(jnp.float32)
    col = lax.broadcasted_iota(jnp.int32, (24, 128), 0)
    present = {0: col >= 4, 3: col < 20}
    count_row = lax.broadcasted_iota(jnp.int32, (8, 128), 0) % 4
    cells = jnp.where((count_row == 0) | (count_row == 3), 20.0, 24.0) * 128.0

    def window(p, t):
        return raw[p, :, 16 * t : 16 * t + 24, :]

    sums = []
    for p in range(2):
        for t in range(4):
            over_rows = jnp.sum(window(p, t), axis=0)
            sums.append(jnp.sum(over_rows, axis=0, keepdims=True))
    center = group_sum(jnp.concatenate(sums, axis=0)) / cells
    sums = []
    for p in range(2):
        for t in range(4):
            at = 4 * p + t
            spread = window(p, t) - center[at : at + 1][None]
            over_rows = jnp.sum(spread * spread, axis=0)
            if t in present:
                over_rows = jnp.where(present[t], over_rows, 0.0)
            sums.append(jnp.sum(over_rows, axis=0, keepdims=True))
    inverse = lax.rsqrt(group_sum(jnp.concatenate(sums, axis=0)) / cells + 1e-06)
    scale = inverse * gain[...]
    offset = shift[...]
    for p in range(2):
        for half in range(2):
            acts = []
            for t in (2 * half, 2 * half + 1):
                at = 4 * p + t
                normed = (window(p, t) - center[at : at + 1][None]) * scale[at : at + 1][None]
                near = 0.5 * (normed + offset[None])
                act = near + near * jnp.tanh(near)
                if t in present:
                    act = jnp.where(present[t][None], act, 0.0)
                acts.append(act)
            joined = jnp.concatenate(acts, axis=1).astype(jnp.bfloat16)
            out[p, :, 48 * half : 48 * half + 48, :] = joined


def weights_body(pos, same, other, same_far, other_far, diag, lower):
    x = pos[1]
    zero = jnp.zeros((32, 128), jnp.bfloat16)
    for b in range(TAPS):
        for e in range(TAPS):
            for core, (near, far) in enumerate(((same, same_far), (other, other_far))):
                for f in range(2):
                    base = e * 256 + core * 128 + f * 64
                    for g in range(2):
                        tap_d, tap_l = f - g + 2, f - g
                        for source, slot in ((near, x), (far, 1 - x)):
                            rows = pl.ds(pl.multiple_of(base + 32 * slot, 32), 32)
                            lanes = slice(128 * g, 128 * g + 128)
                            diag[b, rows, lanes] = source[tap_d, b, e] if tap_d < 3 else zero
                            lower[b, rows, lanes] = source[tap_l, b, e] if tap_l >= 0 else zero


def conv_body(pos, mine, sibling, diag, lower, blend, *refs):
    sends, kept, passed, (stacked, summed, blocks) = refs[:4], refs[4], refs[5], refs[6:]
    z, x = pos[0], pos[1]
    col = lax.broadcasted_iota(jnp.int32, (24, 128), 0)
    for p in range(2):
        edge = jnp.zeros((96, 768), jnp.bfloat16)
        stacked[p, 0:96, :] = edge
        stacked[p, 864:960, :] = edge
        for core, source in enumerate((mine, sibling)):
            act = source[p].reshape(768, 128)
            wide = act.astype(jnp.float32)
            before = pltpu.roll(wide, 1, 0).reshape(32, 24, 128)
            before = jnp.where((col > 0)[None], before, 0.0).reshape(768, 128)
            after = pltpu.roll(wide, 767, 0).reshape(32, 24, 128)
            after = jnp.where((col < 23)[None], after, 0.0).reshape(768, 128)
            lanes = 128 * core
            stacked[p, 96:864, lanes : lanes + 128] = before.astype(jnp.bfloat16)
            stacked[p, 96:864, 256 + lanes : 384 + lanes] = act
            stacked[p, 96:864, 512 + lanes : 640 + lanes] = after.astype(jnp.bfloat16)

    def product(p, b, matrix):
        rows = stacked[p, 96 * b : 96 * b + 768, :]
        return jnp.dot(rows, matrix[b], preferred_element_type=jnp.float32)

    for p in range(2):
        total = sum(product(p, b, diag) for b in range(TAPS))
        if p == 1:
            total = total + sum(product(0, b, lower) for b in range(TAPS))
        total = total.reshape(8, 96, 256)
        for t in range(4):
            start = 24 * t
            left = total[:, start : start + 8]
            if t > 0:
                share = blend[t - 1][None]
                left = share * total[:, start - 8 : start] + (1.0 - share) * left
            summed[:, 16 * t : 16 * t + 8, :] = left
            summed[:, 16 * t + 8 : 16 * t + 16, :] = total[:, start + 8 : start + 16]
        summed[:, 64:72, :] = total[:, 88:96]
        for t in range(4):
            blocks[p, t] = summed[:, 4 + 16 * t : 20 + 16 * t, :]
    for k in range(4):
        sends[k][...] = blocks[1 - x, z ^ k].astype(jnp.bfloat16)
    for i, k in enumerate((0, 2)):
        kept[i] = blocks[x, z ^ k]
        passed[i] = blocks[x, z ^ k ^ 1].astype(jnp.bfloat16)


def add_body(pos, kept, came, *sums):
    for i in range(2):
        sums[i][...] = (kept[i] + came[i].astype(jnp.float32)).astype(sums[i].dtype)


def join_body(pos, bias, own, same, *refs):
    far, out = refs[:4], refs[4]
    x = pos[1]
    near_sum = own[...] + same[...].astype(jnp.float32)
    far_sum = far[0][...].astype(jnp.float32)
    for part in far[1:]:
        far_sum = far_sum + part[...].astype(jnp.float32)
    low = jnp.where(x == 0, near_sum, far_sum)
    high = jnp.where(x == 0, far_sum, near_sum)
    for f in range(2):
        lanes = slice(128 * f, 128 * f + 128)
        out[f, :, :, 0:128] = (low[..., lanes] + bias[:, 0:128][None]).astype(jnp.bfloat16)
        out[f, :, :, 128:256] = (high[..., lanes] + bias[:, 128:256][None]).astype(jnp.bfloat16)


def exchanged(block, k, j):
    tms = lax.axis_size("tm")
    tiles = lax.axis_size("tile")
    route = [(t * tms + m, (t ^ k) * tms + (m ^ j)) for t in range(tiles) for m in range(tms)]
    return lax.ppermute(block, ("tile", "tm"), route)


def across(block, j):
    route = [(2 * m + c, 2 * (m ^ j) + (1 - c)) for m in range(2) for c in range(2)]
    return lax.ppermute(block, ("tm", "ch"), route)


def resident_plan(latent, norm_gain, norm_shift, kernel, conv_bias, blend_profile):
    bf16, f32 = jnp.bfloat16, jnp.float32
    z, x, c = lax.axis_index("tile"), lax.axis_index("tm"), lax.axis_index("ch")
    pos = jnp.stack([z, x]).astype(jnp.int32)
    block = jax.ShapeDtypeStruct((8, 16, 128), bf16)
    wide = jax.ShapeDtypeStruct((8, 16, 256), bf16)

    def quarter(core, frame_block):
        start = core * 256 + frame_block * 128
        return lax.dynamic_slice_in_dim(kernel, start, 128, axis=4)

    quarters = (quarter(c, x), quarter(1 - c, x), quarter(c, 1 - x), quarter(1 - c, 1 - x))
    latent, quarters = lax.optimization_barrier((latent, quarters))
    same = quarters[0]
    other = across(quarters[1], 0)
    same_far = exchanged(quarters[2], 0, 1)
    other_far = across(quarters[3], 1)
    packed = call(pack_body, [block] * 4)(pos, latent)
    near = [packed[0]] + [exchanged(packed[k], k, 0) for k in (1, 2, 3)]
    other_far, near[3] = lax.optimization_barrier((other_far, near[3]))
    far = [exchanged(part, 0, 1) for part in near]
    matrix = jax.ShapeDtypeStruct((TAPS, 768, 256), bf16)
    diag, lower = call(weights_body, [matrix] * 2)(pos, same, other, same_far, other_far)

    def lanes_of(vector):
        part = lax.dynamic_slice_in_dim(vector, z * 64, 64)
        return jnp.concatenate([part, part])[None]

    acts = call(
        norm_body,
        jax.ShapeDtypeStruct((2, 8, 96, 128), bf16),
        [pltpu.VMEM((2, 4, 8, 16, 128), bf16), pltpu.VMEM((2, 8, 72, 128), f32)],
    )(pos, lanes_of(norm_gain), lanes_of(norm_shift), *near, *far)
    sibling = lax.ppermute(acts, "ch", [(0, 1), (1, 0)])

    offsets = jnp.arange(2 * RIM, dtype=jnp.int32)
    ramps = ramp_weight(blend_profile[:3, None], offsets[None, :], RIM)
    blend = jnp.broadcast_to(ramps[:, :, None], (3, 2 * RIM, 256))
    *sends, kept, leaving = call(
        conv_body,
        [wide] * 4 + [jax.ShapeDtypeStruct((2, 8, 16, 256), t) for t in (f32, bf16)],
        [
            pltpu.VMEM((2, 960, 768), bf16),
            pltpu.VMEM((8, 72, 256), f32),
            pltpu.VMEM((2, 4, 8, 16, 256), f32),
        ],
    )(pos, acts, sibling, diag, lower, blend)
    came = exchanged(leaving, 1, 0)
    came, sends[0] = lax.optimization_barrier((came, sends[0]))
    own, leaving = call(add_body, [jax.ShapeDtypeStruct(wide.shape, f32), wide])(pos, kept, came)
    same = exchanged(leaving, 2, 0)
    far = [exchanged(sends[k], k, 1) for k in (3, 2, 0, 1)]
    return call(join_body, jax.ShapeDtypeStruct(latent.shape, bf16))(
        pos, conv_bias[None], own, same, *far
    )


def solution(mesh):
    in_specs = (
        P(("grp", "tm"), None, "tile", "ch"),
        P("ch"),
        P("ch"),
        P(None, None, None, ("ch", "tile", "tm"), None),
        P("ch"),
        P(),
    )
    out_specs = P(("grp", "tm"), None, "tile", "ch")

    def on_device(latent, norm_gain, norm_shift, kernel, conv_bias, blend_profile):
        plan = resident_plan if resident_fits(mesh.shape, latent, kernel) else gathered_plan
        return plan(latent, norm_gain, norm_shift, kernel, conv_bias, blend_profile)

    return jax.shard_map(
        on_device, mesh=mesh, in_specs=in_specs, out_specs=out_specs, check_vma=False
    )
```

```python
import functools

import jax
import jax.numpy as jnp
from jax import lax
from jax.experimental import pallas as pl
from jax.experimental.pallas import tpu as pltpu
from jax.sharding import PartitionSpec as P

GROUPS = 32
RIM = 4
TAPS = 3


def ramp_weight(profile, position, margin):
    fraction = (position.astype(jnp.float32) + 0.5) / (2.0 * margin)
    exponent = 1.0 + profile.astype(jnp.float32)
    near_part = jnp.power(1.0 - fraction, exponent)
    far_part = jnp.power(fraction, exponent)
    return near_part / (near_part + far_part)


def with_halo(shard, sides, width):
    for axis, dim in sides:
        size, length = (lax.axis_size(axis), shard.shape[dim])
        up = [(i, (i + 1) % size) for i in range(size - 1)]
        down = [(j, i) for i, j in up]
        last = lax.slice_in_dim(shard, length - width, length, axis=dim)
        leading = lax.slice_in_dim(shard, 0, width, axis=dim)
        before = lax.ppermute(last, axis, up)
        after = lax.ppermute(leading, axis, down)
        shard = jnp.concatenate([before, shard, after], axis=dim)
    return shard


def passed_along(block, axis, distance):
    devices = range(lax.axis_size(axis))
    route = [(i - distance, i) for i in devices if i - distance in devices]
    return lax.ppermute(block, axis, route)


def frame_stats(values, colmask, groups):
    frame_count, row_count, col_count, chan_count = values.shape
    grouped = values.reshape(frame_count, row_count, col_count, groups, chan_count // groups)
    weight = colmask.reshape(1, 1, col_count, 1, 1)
    counted = row_count * (chan_count // groups) * jnp.sum(colmask)
    center = jnp.sum(grouped * weight, axis=(1, 2, 4)) / counted
    spread = (grouped - center[:, None, None, :, None]) * weight
    inverse = lax.rsqrt(jnp.sum(spread * spread, axis=(1, 2, 4)) / counted + 1e-06)
    return (center, inverse)


def activate(values, center, inverse, norm_gain, norm_shift, colmask, timemask, groups):
    frame_count, row_count, col_count, chan_count = values.shape
    grouped = values.reshape(frame_count, row_count, col_count, groups, chan_count // groups)
    normed = (grouped - center[:, None, None, :, None]) * inverse[:, None, None, :, None]
    normed = normed.reshape(values.shape) * norm_gain + norm_shift
    masked = jax.nn.silu(normed) * colmask[None, None, :, None] * timemask[:, None, None, None]
    return masked.astype(jnp.bfloat16)


def conv_taps(padded, kernel_part, frame_count, row_count, col_count):
    in_width = kernel_part.shape[3]
    running = None
    for tap_time in range(3):
        for tap_row in range(3):
            for tap_col in range(3):
                window = padded[
                    tap_time : tap_time + frame_count,
                    tap_row : tap_row + row_count,
                    tap_col : tap_col + col_count,
                ]
                contrib = jnp.dot(
                    window.reshape(-1, in_width),
                    kernel_part[tap_time, tap_row, tap_col],
                    preferred_element_type=jnp.float32,
                )
                running = contrib if running is None else running + contrib
    return running


def gathered_plan(latent, norm_gain, norm_shift, kernel, conv_bias, blend_profile):
    frame_count, row_count, core_cols, chan_half = latent.shape
    out_chans = kernel.shape[4]
    groups = GROUPS // lax.axis_size("ch")
    ncols = core_cols + 2 * RIM
    tile_pos = lax.axis_index("tile")
    tile_count = lax.axis_size("tile")
    window_in = with_halo(latent, (("tile", 2),), RIM)
    cached = passed_along(window_in, "tm", 1)
    frames = jnp.concatenate([cached, window_in], axis=0).astype(jnp.float32)
    column = tile_pos * core_cols - RIM + jnp.arange(ncols, dtype=jnp.int32)
    colmask = ((column >= 0) & (column < tile_count * core_cols)).astype(jnp.float32)
    started = (lax.axis_index("tm") > 0).astype(jnp.float32)
    timemask = jnp.concatenate(
        [jnp.ones((2,), jnp.float32) * started, jnp.ones((frame_count,), jnp.float32)]
    )
    center, inverse = frame_stats(frames, colmask, groups)
    activated = activate(frames, center, inverse, norm_gain, norm_shift, colmask, timemask, groups)
    padded = jnp.pad(activated, ((0, 0), (1, 1), (1, 1), (0, 0)))
    whole_kernel = lax.all_gather(kernel, ("tile", "tm"), axis=3, tiled=True)
    running = conv_taps(padded, whole_kernel, frame_count, row_count, ncols)
    joined = running.reshape(frame_count, row_count, ncols, out_chans)
    summed = lax.psum_scatter(joined, "ch", scatter_dimension=3, tiled=True)
    tile_out = (summed + conv_bias).astype(jnp.bfloat16)
    extended = with_halo(tile_out, (("tile", 2),), RIM)
    own_out = tile_out[:, :, RIM : RIM + core_cols]
    left_nbr = extended[:, :, :RIM]
    right_nbr = extended[:, :, ncols + RIM :]
    own_profile = lax.dynamic_index_in_dim(blend_profile, tile_pos, 0, keepdims=False)
    prev_profile = lax.dynamic_index_in_dim(
        blend_profile, jnp.maximum(tile_pos - 1, 0), 0, keepdims=False
    )
    offsets = jnp.arange(RIM, dtype=jnp.int32)
    left_weight = jnp.where(tile_pos > 0, ramp_weight(prev_profile, offsets + RIM, RIM), 0.0)
    right_weight = jnp.where(tile_pos < tile_count - 1, ramp_weight(own_profile, offsets, RIM), 1.0)
    left_wide = left_weight[None, None, :, None]
    right_wide = right_weight[None, None, :, None]
    own_float = own_out.astype(jnp.float32)
    head_cols = own_float[:, :, :RIM] * (1.0 - left_wide) + left_nbr.astype(jnp.float32) * left_wide
    tail_cols = own_float[:, :, core_cols - RIM :] * right_wide + right_nbr.astype(jnp.float32) * (
        1.0 - right_wide
    )
    middle = own_float[:, :, RIM : core_cols - RIM]
    return jnp.concatenate([head_cols, middle, tail_cols], axis=2).astype(jnp.bfloat16)


VMEM_BYTES = 48 * 1024 * 1024


def resident_fits(mesh, latent, kernel):
    return (
        mesh["tile"] == 4
        and mesh["tm"] == 2
        and mesh["ch"] == 2
        and latent.shape == (2, 8, 16, 256)
        and kernel.shape == (TAPS, TAPS, TAPS, 32, 512)
    )


def call(body, outs, scratch=(), smem_first=True):
    vmem = pl.BlockSpec(memory_space=pltpu.VMEM)
    smem = pl.BlockSpec(memory_space=pltpu.SMEM)

    def run(*args):
        specs = [smem if smem_first and i == 0 else vmem for i in range(len(args))]
        return pl.pallas_call(
            body,
            out_shape=outs,
            in_specs=specs,
            out_specs=jax.tree.map(lambda _: vmem, outs),
            scratch_shapes=list(scratch),
            compiler_params=pltpu.CompilerParams(vmem_limit_bytes=VMEM_BYTES),
            cost_estimate=pl.CostEstimate(flops=1000, bytes_accessed=1000, transcendentals=0),
        )(*args)

    return run


def pack_body(pos, latent, *outs):
    z = pos[0]
    first = latent[0].astype(jnp.float32)
    second = latent[1].astype(jnp.float32)
    for owner in range(4):
        lanes = slice(64 * owner, 64 * owner + 64)
        block = jnp.concatenate([first[..., lanes], second[..., lanes]], axis=-1)
        block = block.astype(jnp.bfloat16)
        for k in range(4):

            @pl.when(z == owner ^ k)
            def _():
                outs[k][...] = block


def group_sum(rows):
    count = rows.shape[0]
    row = lax.broadcasted_iota(jnp.int32, (128, 128), 0)
    lane = lax.broadcasted_iota(jnp.int32, (128, 128), 1)
    same = (row >> 4 == lane >> 4).astype(jnp.bfloat16)
    terms = []
    for _ in range(3):
        term = rows.astype(jnp.bfloat16)
        terms.append(term.astype(jnp.float32))
        rows = rows - term.astype(jnp.float32)
    terms = jnp.concatenate(terms, axis=0).astype(jnp.bfloat16)
    sums = jnp.dot(terms, same, preferred_element_type=jnp.float32)
    return sums[:count] + sums[count : 2 * count] + sums[2 * count :]


def norm_body(pos, gain, shift, *refs):
    blocks, (out, placed, raw) = refs[:8], refs[8:]
    z, x = pos[0], pos[1]
    for k in range(4):
        placed[x, z ^ k] = blocks[k][...]
        placed[1 - x, z ^ k] = blocks[4 + k][...]
    for p in range(2):
        raw[p, :, 0:4, :] = jnp.zeros((8, 4, 128), jnp.float32)
        raw[p, :, 68:72, :] = jnp.zeros((8, 4, 128), jnp.float32)
        for t in range(4):
            raw[p, :, 4 + 16 * t : 20 + 16 * t, :] = placed[p, t].astype(jnp.float32)
    col = lax.broadcasted_iota(jnp.int32, (24, 128), 0)
    present = {0: col >= 4, 3: col < 20}
    count_row = lax.broadcasted_iota(jnp.int32, (8, 128), 0) % 4
    cells = jnp.where((count_row == 0) | (count_row == 3), 20.0, 24.0) * 128.0

    def window(p, t):
        return raw[p, :, 16 * t : 16 * t + 24, :]

    sums = []
    for p in range(2):
        for t in range(4):
            over_rows = jnp.sum(window(p, t), axis=0)
            sums.append(jnp.sum(over_rows, axis=0, keepdims=True))
    center = group_sum(jnp.concatenate(sums, axis=0)) / cells
    sums = []
    for p in range(2):
        for t in range(4):
            at = 4 * p + t
            spread = window(p, t) - center[at : at + 1][None]
            over_rows = jnp.sum(spread * spread, axis=0)
            if t in present:
                over_rows = jnp.where(present[t], over_rows, 0.0)
            sums.append(jnp.sum(over_rows, axis=0, keepdims=True))
    inverse = lax.rsqrt(group_sum(jnp.concatenate(sums, axis=0)) / cells + 1e-06)
    scale = inverse * gain[...]
    offset = shift[...]
    for p in range(2):
        for half in range(2):
            acts = []
            for t in (2 * half, 2 * half + 1):
                at = 4 * p + t
                normed = (window(p, t) - center[at : at + 1][None]) * scale[at : at + 1][None]
                near = 0.5 * (normed + offset[None])
                act = near + near * jnp.tanh(near)
                if t in present:
                    act = jnp.where(present[t][None], act, 0.0)
                acts.append(act)
            joined = jnp.concatenate(acts, axis=1).astype(jnp.bfloat16)
            out[p, :, 48 * half : 48 * half + 48, :] = joined


def weights_body(pos, same, other, same_far, other_far, diag, lower):
    x = pos[1]
    zero = jnp.zeros((32, 128), jnp.bfloat16)
    for b in range(TAPS):
        for e in range(TAPS):
            for core, (near, far) in enumerate(((same, same_far), (other, other_far))):
                for f in range(2):
                    base = e * 256 + core * 128 + f * 64
                    for g in range(2):
                        tap_d, tap_l = f - g + 2, f - g
                        for source, slot in ((near, x), (far, 1 - x)):
                            rows = pl.ds(pl.multiple_of(base + 32 * slot, 32), 32)
                            lanes = slice(128 * g, 128 * g + 128)
                            diag[b, rows, lanes] = source[tap_d, b, e] if tap_d < 3 else zero
                            lower[b, rows, lanes] = source[tap_l, b, e] if tap_l >= 0 else zero


def conv_body(pos, mine, sibling, diag, lower, blend, *refs):
    sends, kept, passed, (stacked, summed, blocks) = refs[:4], refs[4], refs[5], refs[6:]
    z, x = pos[0], pos[1]
    col = lax.broadcasted_iota(jnp.int32, (24, 128), 0)
    for p in range(2):
        edge = jnp.zeros((96, 768), jnp.bfloat16)
        stacked[p, 0:96, :] = edge
        stacked[p, 864:960, :] = edge
        for core, source in enumerate((mine, sibling)):
            act = source[p].reshape(768, 128)
            wide = act.astype(jnp.float32)
            before = pltpu.roll(wide, 1, 0).reshape(32, 24, 128)
            before = jnp.where((col > 0)[None], before, 0.0).reshape(768, 128)
            after = pltpu.roll(wide, 767, 0).reshape(32, 24, 128)
            after = jnp.where((col < 23)[None], after, 0.0).reshape(768, 128)
            lanes = 128 * core
            stacked[p, 96:864, lanes : lanes + 128] = before.astype(jnp.bfloat16)
            stacked[p, 96:864, 256 + lanes : 384 + lanes] = act
            stacked[p, 96:864, 512 + lanes : 640 + lanes] = after.astype(jnp.bfloat16)

    def product(p, b, matrix):
        rows = stacked[p, 96 * b : 96 * b + 768, :]
        return jnp.dot(rows, matrix[b], preferred_element_type=jnp.float32)

    for p in range(2):
        total = sum(product(p, b, diag) for b in range(TAPS))
        if p == 1:
            total = total + sum(product(0, b, lower) for b in range(TAPS))
        total = total.reshape(8, 96, 256)
        for t in range(4):
            start = 24 * t
            left = total[:, start : start + 8]
            if t > 0:
                share = blend[t - 1][None]
                left = share * total[:, start - 8 : start] + (1.0 - share) * left
            summed[:, 16 * t : 16 * t + 8, :] = left
            summed[:, 16 * t + 8 : 16 * t + 16, :] = total[:, start + 8 : start + 16]
        summed[:, 64:72, :] = total[:, 88:96]
        for t in range(4):
            blocks[p, t] = summed[:, 4 + 16 * t : 20 + 16 * t, :]
    for k in range(4):
        sends[k][...] = blocks[1 - x, z ^ k].astype(jnp.bfloat16)
    for i, k in enumerate((0, 2)):
        kept[i] = blocks[x, z ^ k]
        passed[i] = blocks[x, z ^ k ^ 1].astype(jnp.bfloat16)


def add_body(pos, kept, came, *sums):
    for i in range(2):
        sums[i][...] = (kept[i] + came[i].astype(jnp.float32)).astype(sums[i].dtype)


def join_body(pos, bias, own, same, *refs):
    far, out = refs[:4], refs[4]
    x = pos[1]
    near_sum = own[...] + same[...].astype(jnp.float32)
    far_sum = far[0][...].astype(jnp.float32)
    for part in far[1:]:
        far_sum = far_sum + part[...].astype(jnp.float32)
    low = jnp.where(x == 0, near_sum, far_sum)
    high = jnp.where(x == 0, far_sum, near_sum)
    for f in range(2):
        lanes = slice(128 * f, 128 * f + 128)
        out[f, :, :, 0:128] = (low[..., lanes] + bias[:, 0:128][None]).astype(jnp.bfloat16)
        out[f, :, :, 128:256] = (high[..., lanes] + bias[:, 128:256][None]).astype(jnp.bfloat16)


def exchanged(block, k, j):
    tms = lax.axis_size("tm")
    tiles = lax.axis_size("tile")
    route = [(t * tms + m, (t ^ k) * tms + (m ^ j)) for t in range(tiles) for m in range(tms)]
    return lax.ppermute(block, ("tile", "tm"), route)


def across(block, j):
    route = [(2 * m + c, 2 * (m ^ j) + (1 - c)) for m in range(2) for c in range(2)]
    return lax.ppermute(block, ("tm", "ch"), route)


def resident_plan(latent, norm_gain, norm_shift, kernel, conv_bias, blend_profile):
    bf16, f32 = jnp.bfloat16, jnp.float32
    z, x, c = lax.axis_index("tile"), lax.axis_index("tm"), lax.axis_index("ch")
    pos = jnp.stack([z, x]).astype(jnp.int32)
    block = jax.ShapeDtypeStruct((8, 16, 128), bf16)
    wide = jax.ShapeDtypeStruct((8, 16, 256), bf16)

    def quarter(core, frame_block):
        start = core * 256 + frame_block * 128
        return lax.dynamic_slice_in_dim(kernel, start, 128, axis=4)

    quarters = (quarter(c, x), quarter(1 - c, x), quarter(c, 1 - x), quarter(1 - c, 1 - x))
    latent, quarters = lax.optimization_barrier((latent, quarters))
    same = quarters[0]
    other = across(quarters[1], 0)
    same_far = exchanged(quarters[2], 0, 1)
    other_far = across(quarters[3], 1)
    packed = call(pack_body, [block] * 4)(pos, latent)
    near = [packed[0]] + [exchanged(packed[k], k, 0) for k in (1, 2, 3)]
    same_far, near[3] = lax.optimization_barrier((same_far, near[3]))
    far = [exchanged(part, 0, 1) for part in near]
    matrix = jax.ShapeDtypeStruct((TAPS, 768, 256), bf16)
    diag, lower = call(weights_body, [matrix] * 2)(pos, same, other, same_far, other_far)

    def lanes_of(vector):
        part = lax.dynamic_slice_in_dim(vector, z * 64, 64)
        return jnp.concatenate([part, part])[None]

    acts = call(
        norm_body,
        jax.ShapeDtypeStruct((2, 8, 96, 128), bf16),
        [pltpu.VMEM((2, 4, 8, 16, 128), bf16), pltpu.VMEM((2, 8, 72, 128), f32)],
    )(pos, lanes_of(norm_gain), lanes_of(norm_shift), *near, *far)
    sibling = lax.ppermute(acts, "ch", [(0, 1), (1, 0)])

    offsets = jnp.arange(2 * RIM, dtype=jnp.int32)
    ramps = ramp_weight(blend_profile[:3, None], offsets[None, :], RIM)
    blend = jnp.broadcast_to(ramps[:, :, None], (3, 2 * RIM, 256))
    *sends, kept, leaving = call(
        conv_body,
        [wide] * 4 + [jax.ShapeDtypeStruct((2, 8, 16, 256), t) for t in (f32, bf16)],
        [
            pltpu.VMEM((2, 960, 768), bf16),
            pltpu.VMEM((8, 72, 256), f32),
            pltpu.VMEM((2, 4, 8, 16, 256), f32),
        ],
    )(pos, acts, sibling, diag, lower, blend)
    came = exchanged(leaving, 1, 0)
    came, sends[0] = lax.optimization_barrier((came, sends[0]))
    own, leaving = call(add_body, [jax.ShapeDtypeStruct(wide.shape, f32), wide])(pos, kept, came)
    same = exchanged(leaving, 2, 0)
    far = [exchanged(sends[k], k, 1) for k in (3, 2, 0, 1)]
    return call(join_body, jax.ShapeDtypeStruct(latent.shape, bf16))(
        pos, conv_bias[None], own, same, *far
    )


def solution(mesh):
    in_specs = (
        P(("grp", "tm"), None, "tile", "ch"),
        P("ch"),
        P("ch"),
        P(None, None, None, ("ch", "tile", "tm"), None),
        P("ch"),
        P(),
    )
    out_specs = P(("grp", "tm"), None, "tile", "ch")

    def on_device(latent, norm_gain, norm_shift, kernel, conv_bias, blend_profile):
        plan = resident_plan if resident_fits(mesh.shape, latent, kernel) else gathered_plan
        return plan(latent, norm_gain, norm_shift, kernel, conv_bias, blend_profile)

    return jax.shard_map(
        on_device, mesh=mesh, in_specs=in_specs, out_specs=out_specs, check_vma=False
    )
```

```python
import functools

import jax
import jax.numpy as jnp
from jax import lax
from jax.experimental import pallas as pl
from jax.experimental.pallas import tpu as pltpu
from jax.sharding import PartitionSpec as P

GROUPS = 32
RIM = 4
TAPS = 3


def ramp_weight(profile, position, margin):
    fraction = (position.astype(jnp.float32) + 0.5) / (2.0 * margin)
    exponent = 1.0 + profile.astype(jnp.float32)
    near_part = jnp.power(1.0 - fraction, exponent)
    far_part = jnp.power(fraction, exponent)
    return near_part / (near_part + far_part)


def with_halo(shard, sides, width):
    for axis, dim in sides:
        size, length = (lax.axis_size(axis), shard.shape[dim])
        up = [(i, (i + 1) % size) for i in range(size - 1)]
        down = [(j, i) for i, j in up]
        last = lax.slice_in_dim(shard, length - width, length, axis=dim)
        leading = lax.slice_in_dim(shard, 0, width, axis=dim)
        before = lax.ppermute(last, axis, up)
        after = lax.ppermute(leading, axis, down)
        shard = jnp.concatenate([before, shard, after], axis=dim)
    return shard


def passed_along(block, axis, distance):
    devices = range(lax.axis_size(axis))
    route = [(i - distance, i) for i in devices if i - distance in devices]
    return lax.ppermute(block, axis, route)


def frame_stats(values, colmask, groups):
    frame_count, row_count, col_count, chan_count = values.shape
    grouped = values.reshape(frame_count, row_count, col_count, groups, chan_count // groups)
    weight = colmask.reshape(1, 1, col_count, 1, 1)
    counted = row_count * (chan_count // groups) * jnp.sum(colmask)
    center = jnp.sum(grouped * weight, axis=(1, 2, 4)) / counted
    spread = (grouped - center[:, None, None, :, None]) * weight
    inverse = lax.rsqrt(jnp.sum(spread * spread, axis=(1, 2, 4)) / counted + 1e-06)
    return (center, inverse)


def activate(values, center, inverse, norm_gain, norm_shift, colmask, timemask, groups):
    frame_count, row_count, col_count, chan_count = values.shape
    grouped = values.reshape(frame_count, row_count, col_count, groups, chan_count // groups)
    normed = (grouped - center[:, None, None, :, None]) * inverse[:, None, None, :, None]
    normed = normed.reshape(values.shape) * norm_gain + norm_shift
    masked = jax.nn.silu(normed) * colmask[None, None, :, None] * timemask[:, None, None, None]
    return masked.astype(jnp.bfloat16)


def conv_taps(padded, kernel_part, frame_count, row_count, col_count):
    in_width = kernel_part.shape[3]
    running = None
    for tap_time in range(3):
        for tap_row in range(3):
            for tap_col in range(3):
                window = padded[
                    tap_time : tap_time + frame_count,
                    tap_row : tap_row + row_count,
                    tap_col : tap_col + col_count,
                ]
                contrib = jnp.dot(
                    window.reshape(-1, in_width),
                    kernel_part[tap_time, tap_row, tap_col],
                    preferred_element_type=jnp.float32,
                )
                running = contrib if running is None else running + contrib
    return running


def gathered_plan(latent, norm_gain, norm_shift, kernel, conv_bias, blend_profile):
    frame_count, row_count, core_cols, chan_half = latent.shape
    out_chans = kernel.shape[4]
    groups = GROUPS // lax.axis_size("ch")
    ncols = core_cols + 2 * RIM
    tile_pos = lax.axis_index("tile")
    tile_count = lax.axis_size("tile")
    window_in = with_halo(latent, (("tile", 2),), RIM)
    cached = passed_along(window_in, "tm", 1)
    frames = jnp.concatenate([cached, window_in], axis=0).astype(jnp.float32)
    column = tile_pos * core_cols - RIM + jnp.arange(ncols, dtype=jnp.int32)
    colmask = ((column >= 0) & (column < tile_count * core_cols)).astype(jnp.float32)
    started = (lax.axis_index("tm") > 0).astype(jnp.float32)
    timemask = jnp.concatenate(
        [jnp.ones((2,), jnp.float32) * started, jnp.ones((frame_count,), jnp.float32)]
    )
    center, inverse = frame_stats(frames, colmask, groups)
    activated = activate(frames, center, inverse, norm_gain, norm_shift, colmask, timemask, groups)
    padded = jnp.pad(activated, ((0, 0), (1, 1), (1, 1), (0, 0)))
    whole_kernel = lax.all_gather(kernel, ("tile", "tm"), axis=3, tiled=True)
    running = conv_taps(padded, whole_kernel, frame_count, row_count, ncols)
    joined = running.reshape(frame_count, row_count, ncols, out_chans)
    summed = lax.psum_scatter(joined, "ch", scatter_dimension=3, tiled=True)
    tile_out = (summed + conv_bias).astype(jnp.bfloat16)
    extended = with_halo(tile_out, (("tile", 2),), RIM)
    own_out = tile_out[:, :, RIM : RIM + core_cols]
    left_nbr = extended[:, :, :RIM]
    right_nbr = extended[:, :, ncols + RIM :]
    own_profile = lax.dynamic_index_in_dim(blend_profile, tile_pos, 0, keepdims=False)
    prev_profile = lax.dynamic_index_in_dim(
        blend_profile, jnp.maximum(tile_pos - 1, 0), 0, keepdims=False
    )
    offsets = jnp.arange(RIM, dtype=jnp.int32)
    left_weight = jnp.where(tile_pos > 0, ramp_weight(prev_profile, offsets + RIM, RIM), 0.0)
    right_weight = jnp.where(tile_pos < tile_count - 1, ramp_weight(own_profile, offsets, RIM), 1.0)
    left_wide = left_weight[None, None, :, None]
    right_wide = right_weight[None, None, :, None]
    own_float = own_out.astype(jnp.float32)
    head_cols = own_float[:, :, :RIM] * (1.0 - left_wide) + left_nbr.astype(jnp.float32) * left_wide
    tail_cols = own_float[:, :, core_cols - RIM :] * right_wide + right_nbr.astype(jnp.float32) * (
        1.0 - right_wide
    )
    middle = own_float[:, :, RIM : core_cols - RIM]
    return jnp.concatenate([head_cols, middle, tail_cols], axis=2).astype(jnp.bfloat16)


VMEM_BYTES = 24 * 1024 * 1024


def resident_fits(mesh, latent, kernel):
    return (
        mesh["tile"] == 4
        and mesh["tm"] == 2
        and mesh["ch"] == 2
        and latent.shape == (2, 8, 16, 256)
        and kernel.shape == (TAPS, TAPS, TAPS, 32, 512)
    )


def call(body, outs, scratch=(), smem_first=True):
    vmem = pl.BlockSpec(memory_space=pltpu.VMEM)
    smem = pl.BlockSpec(memory_space=pltpu.SMEM)

    def run(*args):
        specs = [smem if smem_first and i == 0 else vmem for i in range(len(args))]
        return pl.pallas_call(
            body,
            out_shape=outs,
            in_specs=specs,
            out_specs=jax.tree.map(lambda _: vmem, outs),
            scratch_shapes=list(scratch),
            compiler_params=pltpu.CompilerParams(vmem_limit_bytes=VMEM_BYTES),
            cost_estimate=pl.CostEstimate(flops=1000, bytes_accessed=1000, transcendentals=0),
        )(*args)

    return run


def pack_body(pos, latent, *refs):
    outs, packed = refs[:4], refs[4]
    z = pos[0]
    first = latent[0].astype(jnp.float32)
    second = latent[1].astype(jnp.float32)
    for owner in range(4):
        lanes = slice(64 * owner, 64 * owner + 64)
        block = jnp.concatenate([first[..., lanes], second[..., lanes]], axis=-1)
        packed[owner] = block.astype(jnp.bfloat16)
    for k in range(4):
        outs[k][...] = packed[z ^ k]


def group_sum(rows):
    count = rows.shape[0]
    row = lax.broadcasted_iota(jnp.int32, (128, 128), 0)
    lane = lax.broadcasted_iota(jnp.int32, (128, 128), 1)
    same = (row >> 4 == lane >> 4).astype(jnp.bfloat16)
    terms = []
    for _ in range(3):
        term = rows.astype(jnp.bfloat16)
        terms.append(term.astype(jnp.float32))
        rows = rows - term.astype(jnp.float32)
    terms = jnp.concatenate(terms, axis=0).astype(jnp.bfloat16)
    sums = jnp.dot(terms, same, preferred_element_type=jnp.float32)
    return sums[:count] + sums[count : 2 * count] + sums[2 * count :]


def norm_body(pos, gain, shift, *refs):
    blocks, (out, placed, raw) = refs[:8], refs[8:]
    z, x = pos[0], pos[1]
    for k in range(4):
        placed[x, z ^ k] = blocks[k][...]
        placed[1 - x, z ^ k] = blocks[4 + k][...]
    for p in range(2):
        raw[p, :, 0:4, :] = jnp.zeros((8, 4, 128), jnp.float32)
        raw[p, :, 68:72, :] = jnp.zeros((8, 4, 128), jnp.float32)
        for t in range(4):
            raw[p, :, 4 + 16 * t : 20 + 16 * t, :] = placed[p, t].astype(jnp.float32)
    col = lax.broadcasted_iota(jnp.int32, (24, 128), 0)
    present = {0: col >= 4, 3: col < 20}
    count_row = lax.broadcasted_iota(jnp.int32, (8, 128), 0) % 4
    cells = jnp.where((count_row == 0) | (count_row == 3), 20.0, 24.0) * 128.0

    def window(p, t):
        return raw[p, :, 16 * t : 16 * t + 24, :]

    sums = []
    for p in range(2):
        for t in range(4):
            over_rows = jnp.sum(window(p, t), axis=0)
            sums.append(jnp.sum(over_rows, axis=0, keepdims=True))
    center = group_sum(jnp.concatenate(sums, axis=0)) / cells
    sums = []
    for p in range(2):
        for t in range(4):
            at = 4 * p + t
            spread = window(p, t) - center[at : at + 1][None]
            over_rows = jnp.sum(spread * spread, axis=0)
            if t in present:
                over_rows = jnp.where(present[t], over_rows, 0.0)
            sums.append(jnp.sum(over_rows, axis=0, keepdims=True))
    inverse = lax.rsqrt(group_sum(jnp.concatenate(sums, axis=0)) / cells + 1e-06)
    scale = inverse * gain[...]
    offset = shift[...]
    for p in range(2):
        for half in range(2):
            acts = []
            for t in (2 * half, 2 * half + 1):
                at = 4 * p + t
                normed = (window(p, t) - center[at : at + 1][None]) * scale[at : at + 1][None]
                near = 0.5 * (normed + offset[None])
                act = near + near * jnp.tanh(near)
                if t in present:
                    act = jnp.where(present[t][None], act, 0.0)
                acts.append(act)
            joined = jnp.concatenate(acts, axis=1).astype(jnp.bfloat16)
            out[p, :, 48 * half : 48 * half + 48, :] = joined


def weights_body(pos, same, other, same_far, other_far, diag, lower):
    x = pos[1]
    zero = jnp.zeros((32, 128), jnp.bfloat16)
    for b in range(TAPS):
        for e in range(TAPS):
            for core, (near, far) in enumerate(((same, same_far), (other, other_far))):
                for f in range(2):
                    base = e * 256 + core * 128 + f * 64
                    for g in range(2):
                        tap_d, tap_l = f - g + 2, f - g
                        for source, slot in ((near, x), (far, 1 - x)):
                            rows = pl.ds(pl.multiple_of(base + 32 * slot, 32), 32)
                            lanes = slice(128 * g, 128 * g + 128)
                            diag[b, rows, lanes] = source[tap_d, b, e] if tap_d < 3 else zero
                            lower[b, rows, lanes] = source[tap_l, b, e] if tap_l >= 0 else zero


def conv_body(pos, mine, sibling, diag, lower, blend, *refs):
    sends, kept, passed, (stacked, summed, blocks) = refs[:4], refs[4], refs[5], refs[6:]
    z, x = pos[0], pos[1]
    col = lax.broadcasted_iota(jnp.int32, (24, 128), 0)
    for p in range(2):
        edge = jnp.zeros((96, 768), jnp.bfloat16)
        stacked[p, 0:96, :] = edge
        stacked[p, 864:960, :] = edge
        for core, source in enumerate((mine, sibling)):
            act = source[p].reshape(768, 128)
            wide = act.astype(jnp.float32)
            before = pltpu.roll(wide, 1, 0).reshape(32, 24, 128)
            before = jnp.where((col > 0)[None], before, 0.0).reshape(768, 128)
            after = pltpu.roll(wide, 767, 0).reshape(32, 24, 128)
            after = jnp.where((col < 23)[None], after, 0.0).reshape(768, 128)
            lanes = 128 * core
            stacked[p, 96:864, lanes : lanes + 128] = before.astype(jnp.bfloat16)
            stacked[p, 96:864, 256 + lanes : 384 + lanes] = act
            stacked[p, 96:864, 512 + lanes : 640 + lanes] = after.astype(jnp.bfloat16)

    def product(p, b, matrix):
        rows = stacked[p, 96 * b : 96 * b + 768, :]
        return jnp.dot(rows, matrix[b], preferred_element_type=jnp.float32)

    for p in range(2):
        total = sum(product(p, b, diag) for b in range(TAPS))
        if p == 1:
            total = total + sum(product(0, b, lower) for b in range(TAPS))
        total = total.reshape(8, 96, 256)
        for t in range(4):
            start = 24 * t
            left = total[:, start : start + 8]
            if t > 0:
                share = blend[t - 1][None]
                left = share * total[:, start - 8 : start] + (1.0 - share) * left
            summed[:, 16 * t : 16 * t + 8, :] = left
            summed[:, 16 * t + 8 : 16 * t + 16, :] = total[:, start + 8 : start + 16]
        summed[:, 64:72, :] = total[:, 88:96]
        for t in range(4):
            blocks[p, t] = summed[:, 4 + 16 * t : 20 + 16 * t, :]
    for k in range(4):
        sends[k][...] = blocks[1 - x, z ^ k].astype(jnp.bfloat16)
    for i, k in enumerate((0, 2)):
        kept[i] = blocks[x, z ^ k]
        passed[i] = blocks[x, z ^ k ^ 1].astype(jnp.bfloat16)


def add_body(pos, kept, came, *sums):
    for i in range(2):
        sums[i][...] = (kept[i] + came[i].astype(jnp.float32)).astype(sums[i].dtype)


def join_body(pos, bias, own, same, *refs):
    far, out = refs[:4], refs[4]
    x = pos[1]
    near_sum = own[...] + same[...].astype(jnp.float32)
    far_sum = far[0][...].astype(jnp.float32)
    for part in far[1:]:
        far_sum = far_sum + part[...].astype(jnp.float32)
    low = jnp.where(x == 0, near_sum, far_sum)
    high = jnp.where(x == 0, far_sum, near_sum)
    for f in range(2):
        lanes = slice(128 * f, 128 * f + 128)
        out[f, :, :, 0:128] = (low[..., lanes] + bias[:, 0:128][None]).astype(jnp.bfloat16)
        out[f, :, :, 128:256] = (high[..., lanes] + bias[:, 128:256][None]).astype(jnp.bfloat16)


def exchanged(block, k, j):
    tms = lax.axis_size("tm")
    tiles = lax.axis_size("tile")
    route = [(t * tms + m, (t ^ k) * tms + (m ^ j)) for t in range(tiles) for m in range(tms)]
    return lax.ppermute(block, ("tile", "tm"), route)


def across(block, j):
    route = [(2 * m + c, 2 * (m ^ j) + (1 - c)) for m in range(2) for c in range(2)]
    return lax.ppermute(block, ("tm", "ch"), route)


def resident_plan(latent, norm_gain, norm_shift, kernel, conv_bias, blend_profile):
    bf16, f32 = jnp.bfloat16, jnp.float32
    z, x, c = lax.axis_index("tile"), lax.axis_index("tm"), lax.axis_index("ch")
    pos = jnp.stack([z, x]).astype(jnp.int32)
    block = jax.ShapeDtypeStruct((8, 16, 128), bf16)
    wide = jax.ShapeDtypeStruct((8, 16, 256), bf16)

    def quarter(core, frame_block):
        start = core * 256 + frame_block * 128
        return lax.dynamic_slice_in_dim(kernel, start, 128, axis=4)

    quarters = (quarter(c, x), quarter(1 - c, x), quarter(c, 1 - x), quarter(1 - c, 1 - x))
    latent, quarters = lax.optimization_barrier((latent, quarters))
    same = quarters[0]
    other = across(quarters[1], 0)
    same_far = exchanged(quarters[2], 0, 1)
    other_far = across(quarters[3], 1)
    packed = call(pack_body, [block] * 4, [pltpu.VMEM((4, 8, 16, 128), bf16)])(pos, latent)
    near = [packed[0]] + [exchanged(packed[k], k, 0) for k in (1, 2, 3)]
    same_far, near[3] = lax.optimization_barrier((same_far, near[3]))
    far = [exchanged(part, 0, 1) for part in near]
    matrix = jax.ShapeDtypeStruct((TAPS, 768, 256), bf16)
    diag, lower = call(weights_body, [matrix] * 2)(pos, same, other, same_far, other_far)

    def lanes_of(vector):
        part = lax.dynamic_slice_in_dim(vector, z * 64, 64)
        return jnp.concatenate([part, part])[None]

    acts = call(
        norm_body,
        jax.ShapeDtypeStruct((2, 8, 96, 128), bf16),
        [pltpu.VMEM((2, 4, 8, 16, 128), bf16), pltpu.VMEM((2, 8, 72, 128), f32)],
    )(pos, lanes_of(norm_gain), lanes_of(norm_shift), *near, *far)
    sibling = lax.ppermute(acts, "ch", [(0, 1), (1, 0)])

    offsets = jnp.arange(2 * RIM, dtype=jnp.int32)
    ramps = ramp_weight(blend_profile[:3, None], offsets[None, :], RIM)
    blend = jnp.broadcast_to(ramps[:, :, None], (3, 2 * RIM, 256))
    *sends, kept, leaving = call(
        conv_body,
        [wide] * 4 + [jax.ShapeDtypeStruct((2, 8, 16, 256), t) for t in (f32, bf16)],
        [
            pltpu.VMEM((2, 960, 768), bf16),
            pltpu.VMEM((8, 72, 256), f32),
            pltpu.VMEM((2, 4, 8, 16, 256), f32),
        ],
    )(pos, acts, sibling, diag, lower, blend)
    came = exchanged(leaving, 1, 0)
    came, sends[0] = lax.optimization_barrier((came, sends[0]))
    own, leaving = call(add_body, [jax.ShapeDtypeStruct(wide.shape, f32), wide])(pos, kept, came)
    same = exchanged(leaving, 2, 0)
    far = [exchanged(sends[k], k, 1) for k in (3, 2, 0, 1)]
    return call(join_body, jax.ShapeDtypeStruct(latent.shape, bf16))(
        pos, conv_bias[None], own, same, *far
    )


def solution(mesh):
    in_specs = (
        P(("grp", "tm"), None, "tile", "ch"),
        P("ch"),
        P("ch"),
        P(None, None, None, ("ch", "tile", "tm"), None),
        P("ch"),
        P(),
    )
    out_specs = P(("grp", "tm"), None, "tile", "ch")

    def on_device(latent, norm_gain, norm_shift, kernel, conv_bias, blend_profile):
        plan = resident_plan if resident_fits(mesh.shape, latent, kernel) else gathered_plan
        return plan(latent, norm_gain, norm_shift, kernel, conv_bias, blend_profile)

    return jax.shard_map(
        on_device, mesh=mesh, in_specs=in_specs, out_specs=out_specs, check_vma=False
    )
```

```python
import functools

import jax
import jax.numpy as jnp
from jax import lax
from jax.experimental import pallas as pl
from jax.experimental.pallas import tpu as pltpu
from jax.sharding import PartitionSpec as P

GROUPS = 32
RIM = 4
TAPS = 3


def ramp_weight(profile, position, margin):
    fraction = (position.astype(jnp.float32) + 0.5) / (2.0 * margin)
    exponent = 1.0 + profile.astype(jnp.float32)
    near_part = jnp.power(1.0 - fraction, exponent)
    far_part = jnp.power(fraction, exponent)
    return near_part / (near_part + far_part)


def with_halo(shard, sides, width):
    for axis, dim in sides:
        size, length = (lax.axis_size(axis), shard.shape[dim])
        up = [(i, (i + 1) % size) for i in range(size - 1)]
        down = [(j, i) for i, j in up]
        last = lax.slice_in_dim(shard, length - width, length, axis=dim)
        leading = lax.slice_in_dim(shard, 0, width, axis=dim)
        before = lax.ppermute(last, axis, up)
        after = lax.ppermute(leading, axis, down)
        shard = jnp.concatenate([before, shard, after], axis=dim)
    return shard


def passed_along(block, axis, distance):
    devices = range(lax.axis_size(axis))
    route = [(i - distance, i) for i in devices if i - distance in devices]
    return lax.ppermute(block, axis, route)


def frame_stats(values, colmask, groups):
    frame_count, row_count, col_count, chan_count = values.shape
    grouped = values.reshape(frame_count, row_count, col_count, groups, chan_count // groups)
    weight = colmask.reshape(1, 1, col_count, 1, 1)
    counted = row_count * (chan_count // groups) * jnp.sum(colmask)
    center = jnp.sum(grouped * weight, axis=(1, 2, 4)) / counted
    spread = (grouped - center[:, None, None, :, None]) * weight
    inverse = lax.rsqrt(jnp.sum(spread * spread, axis=(1, 2, 4)) / counted + 1e-06)
    return (center, inverse)


def activate(values, center, inverse, norm_gain, norm_shift, colmask, timemask, groups):
    frame_count, row_count, col_count, chan_count = values.shape
    grouped = values.reshape(frame_count, row_count, col_count, groups, chan_count // groups)
    normed = (grouped - center[:, None, None, :, None]) * inverse[:, None, None, :, None]
    normed = normed.reshape(values.shape) * norm_gain + norm_shift
    masked = jax.nn.silu(normed) * colmask[None, None, :, None] * timemask[:, None, None, None]
    return masked.astype(jnp.bfloat16)


def conv_taps(padded, kernel_part, frame_count, row_count, col_count):
    in_width = kernel_part.shape[3]
    running = None
    for tap_time in range(3):
        for tap_row in range(3):
            for tap_col in range(3):
                window = padded[
                    tap_time : tap_time + frame_count,
                    tap_row : tap_row + row_count,
                    tap_col : tap_col + col_count,
                ]
                contrib = jnp.dot(
                    window.reshape(-1, in_width),
                    kernel_part[tap_time, tap_row, tap_col],
                    preferred_element_type=jnp.float32,
                )
                running = contrib if running is None else running + contrib
    return running


def gathered_plan(latent, norm_gain, norm_shift, kernel, conv_bias, blend_profile):
    frame_count, row_count, core_cols, chan_half = latent.shape
    out_chans = kernel.shape[4]
    groups = GROUPS // lax.axis_size("ch")
    ncols = core_cols + 2 * RIM
    tile_pos = lax.axis_index("tile")
    tile_count = lax.axis_size("tile")
    window_in = with_halo(latent, (("tile", 2),), RIM)
    cached = passed_along(window_in, "tm", 1)
    frames = jnp.concatenate([cached, window_in], axis=0).astype(jnp.float32)
    column = tile_pos * core_cols - RIM + jnp.arange(ncols, dtype=jnp.int32)
    colmask = ((column >= 0) & (column < tile_count * core_cols)).astype(jnp.float32)
    started = (lax.axis_index("tm") > 0).astype(jnp.float32)
    timemask = jnp.concatenate(
        [jnp.ones((2,), jnp.float32) * started, jnp.ones((frame_count,), jnp.float32)]
    )
    center, inverse = frame_stats(frames, colmask, groups)
    activated = activate(frames, center, inverse, norm_gain, norm_shift, colmask, timemask, groups)
    padded = jnp.pad(activated, ((0, 0), (1, 1), (1, 1), (0, 0)))
    whole_kernel = lax.all_gather(kernel, ("tile", "tm"), axis=3, tiled=True)
    running = conv_taps(padded, whole_kernel, frame_count, row_count, ncols)
    joined = running.reshape(frame_count, row_count, ncols, out_chans)
    summed = lax.psum_scatter(joined, "ch", scatter_dimension=3, tiled=True)
    tile_out = (summed + conv_bias).astype(jnp.bfloat16)
    extended = with_halo(tile_out, (("tile", 2),), RIM)
    own_out = tile_out[:, :, RIM : RIM + core_cols]
    left_nbr = extended[:, :, :RIM]
    right_nbr = extended[:, :, ncols + RIM :]
    own_profile = lax.dynamic_index_in_dim(blend_profile, tile_pos, 0, keepdims=False)
    prev_profile = lax.dynamic_index_in_dim(
        blend_profile, jnp.maximum(tile_pos - 1, 0), 0, keepdims=False
    )
    offsets = jnp.arange(RIM, dtype=jnp.int32)
    left_weight = jnp.where(tile_pos > 0, ramp_weight(prev_profile, offsets + RIM, RIM), 0.0)
    right_weight = jnp.where(tile_pos < tile_count - 1, ramp_weight(own_profile, offsets, RIM), 1.0)
    left_wide = left_weight[None, None, :, None]
    right_wide = right_weight[None, None, :, None]
    own_float = own_out.astype(jnp.float32)
    head_cols = own_float[:, :, :RIM] * (1.0 - left_wide) + left_nbr.astype(jnp.float32) * left_wide
    tail_cols = own_float[:, :, core_cols - RIM :] * right_wide + right_nbr.astype(jnp.float32) * (
        1.0 - right_wide
    )
    middle = own_float[:, :, RIM : core_cols - RIM]
    return jnp.concatenate([head_cols, middle, tail_cols], axis=2).astype(jnp.bfloat16)


VMEM_BYTES = 24 * 1024 * 1024


def resident_fits(mesh, latent, kernel):
    return (
        mesh["tile"] == 4
        and mesh["tm"] == 2
        and mesh["ch"] == 2
        and latent.shape == (2, 8, 16, 256)
        and kernel.shape == (TAPS, TAPS, TAPS, 32, 512)
    )


def call(body, outs, scratch=(), smem_first=True):
    vmem = pl.BlockSpec(memory_space=pltpu.VMEM)
    smem = pl.BlockSpec(memory_space=pltpu.SMEM)

    def run(*args):
        specs = [smem if smem_first and i == 0 else vmem for i in range(len(args))]
        return pl.pallas_call(
            body,
            out_shape=outs,
            in_specs=specs,
            out_specs=jax.tree.map(lambda _: vmem, outs),
            scratch_shapes=list(scratch),
            compiler_params=pltpu.CompilerParams(vmem_limit_bytes=VMEM_BYTES),
            cost_estimate=pl.CostEstimate(flops=1000, bytes_accessed=1000, transcendentals=0),
        )(*args)

    return run


def pack_body(pos, latent, *refs):
    outs, packed = refs[:4], refs[4]
    z = pos[0]
    first = latent[0].astype(jnp.float32)
    second = latent[1].astype(jnp.float32)
    for owner in range(4):
        lanes = slice(64 * owner, 64 * owner + 64)
        block = jnp.concatenate([first[..., lanes], second[..., lanes]], axis=-1)
        packed[owner] = block.astype(jnp.bfloat16)
    for k in range(4):
        outs[k][...] = packed[z ^ k]


def group_sum(rows):
    count = rows.shape[0]
    row = lax.broadcasted_iota(jnp.int32, (128, 128), 0)
    lane = lax.broadcasted_iota(jnp.int32, (128, 128), 1)
    same = (row >> 4 == lane >> 4).astype(jnp.bfloat16)
    terms = []
    for _ in range(3):
        term = rows.astype(jnp.bfloat16)
        terms.append(term.astype(jnp.float32))
        rows = rows - term.astype(jnp.float32)
    terms = jnp.concatenate(terms, axis=0).astype(jnp.bfloat16)
    sums = jnp.dot(terms, same, preferred_element_type=jnp.float32)
    return sums[:count] + sums[count : 2 * count] + sums[2 * count :]


NORM = (0, 1, 3, 2)


def norm_body(pos, gain, shift, *refs):
    blocks, (out, placed, raw) = refs[:8], refs[8:]
    z, x = pos[0], pos[1]
    for i, k in enumerate(NORM):
        placed[x, z ^ k] = blocks[i][...]
        placed[1 - x, z ^ k] = blocks[4 + i][...]
    for p in range(2):
        raw[p, :, 0:4, :] = jnp.zeros((8, 4, 128), jnp.float32)
        raw[p, :, 68:72, :] = jnp.zeros((8, 4, 128), jnp.float32)
        for t in range(4):
            raw[p, :, 4 + 16 * t : 20 + 16 * t, :] = placed[p, t].astype(jnp.float32)
    col = lax.broadcasted_iota(jnp.int32, (24, 128), 0)
    present = {0: col >= 4, 3: col < 20}
    count_row = lax.broadcasted_iota(jnp.int32, (8, 128), 0) % 4
    cells = jnp.where((count_row == 0) | (count_row == 3), 20.0, 24.0) * 128.0

    def window(p, t):
        return raw[p, :, 16 * t : 16 * t + 24, :]

    sums = []
    for p in range(2):
        for t in range(4):
            over_rows = jnp.sum(window(p, t), axis=0)
            sums.append(jnp.sum(over_rows, axis=0, keepdims=True))
    center = group_sum(jnp.concatenate(sums, axis=0)) / cells
    sums = []
    for p in range(2):
        for t in range(4):
            at = 4 * p + t
            spread = window(p, t) - center[at : at + 1][None]
            over_rows = jnp.sum(spread * spread, axis=0)
            if t in present:
                over_rows = jnp.where(present[t], over_rows, 0.0)
            sums.append(jnp.sum(over_rows, axis=0, keepdims=True))
    inverse = lax.rsqrt(group_sum(jnp.concatenate(sums, axis=0)) / cells + 1e-06)
    scale = inverse * gain[...]
    offset = shift[...]
    for p in range(2):
        for half in range(2):
            acts = []
            for t in (2 * half, 2 * half + 1):
                at = 4 * p + t
                normed = (window(p, t) - center[at : at + 1][None]) * scale[at : at + 1][None]
                near = 0.5 * (normed + offset[None])
                act = near + near * jnp.tanh(near)
                if t in present:
                    act = jnp.where(present[t][None], act, 0.0)
                acts.append(act)
            joined = jnp.concatenate(acts, axis=1).astype(jnp.bfloat16)
            out[p, :, 48 * half : 48 * half + 48, :] = joined


def weights_body(pos, same, other, same_far, other_far, diag, lower):
    x = pos[1]
    zero = jnp.zeros((32, 128), jnp.bfloat16)
    for b in range(TAPS):
        for e in range(TAPS):
            for core, (near, far) in enumerate(((same, same_far), (other, other_far))):
                for f in range(2):
                    base = e * 256 + core * 128 + f * 64
                    for g in range(2):
                        tap_d, tap_l = f - g + 2, f - g
                        for source, slot in ((near, x), (far, 1 - x)):
                            rows = pl.ds(pl.multiple_of(base + 32 * slot, 32), 32)
                            lanes = slice(128 * g, 128 * g + 128)
                            diag[b, rows, lanes] = source[tap_d, b, e] if tap_d < 3 else zero
                            lower[b, rows, lanes] = source[tap_l, b, e] if tap_l >= 0 else zero


def conv_body(pos, mine, sibling, diag, lower, blend, *refs):
    sends, kept, passed, (stacked, summed, blocks) = refs[:4], refs[4], refs[5], refs[6:]
    z, x = pos[0], pos[1]
    col = lax.broadcasted_iota(jnp.int32, (24, 128), 0)
    for p in range(2):
        edge = jnp.zeros((96, 768), jnp.bfloat16)
        stacked[p, 0:96, :] = edge
        stacked[p, 864:960, :] = edge
        for core, source in enumerate((mine, sibling)):
            act = source[p].reshape(768, 128)
            wide = act.astype(jnp.float32)
            before = pltpu.roll(wide, 1, 0).reshape(32, 24, 128)
            before = jnp.where((col > 0)[None], before, 0.0).reshape(768, 128)
            after = pltpu.roll(wide, 767, 0).reshape(32, 24, 128)
            after = jnp.where((col < 23)[None], after, 0.0).reshape(768, 128)
            lanes = 128 * core
            stacked[p, 96:864, lanes : lanes + 128] = before.astype(jnp.bfloat16)
            stacked[p, 96:864, 256 + lanes : 384 + lanes] = act
            stacked[p, 96:864, 512 + lanes : 640 + lanes] = after.astype(jnp.bfloat16)

    def product(p, b, matrix):
        rows = stacked[p, 96 * b : 96 * b + 768, :]
        return jnp.dot(rows, matrix[b], preferred_element_type=jnp.float32)

    for p in range(2):
        total = sum(product(p, b, diag) for b in range(TAPS))
        if p == 1:
            total = total + sum(product(0, b, lower) for b in range(TAPS))
        total = total.reshape(8, 96, 256)
        for t in range(4):
            start = 24 * t
            left = total[:, start : start + 8]
            if t > 0:
                share = blend[t - 1][None]
                left = share * total[:, start - 8 : start] + (1.0 - share) * left
            summed[:, 16 * t : 16 * t + 8, :] = left
            summed[:, 16 * t + 8 : 16 * t + 16, :] = total[:, start + 8 : start + 16]
        summed[:, 64:72, :] = total[:, 88:96]
        for t in range(4):
            blocks[p, t] = summed[:, 4 + 16 * t : 20 + 16 * t, :]
    for k in range(4):
        sends[k][...] = blocks[1 - x, z ^ k].astype(jnp.bfloat16)
    for i, k in enumerate((0, 2)):
        kept[i] = blocks[x, z ^ k]
        passed[i] = blocks[x, z ^ k ^ 1].astype(jnp.bfloat16)


def add_body(pos, kept, came, *sums):
    for i in range(2):
        sums[i][...] = (kept[i] + came[i].astype(jnp.float32)).astype(sums[i].dtype)


def join_body(pos, bias, own, same, *refs):
    far, out = refs[:4], refs[4]
    x = pos[1]
    near_sum = own[...] + same[...].astype(jnp.float32)
    far_sum = far[0][...].astype(jnp.float32)
    for part in far[1:]:
        far_sum = far_sum + part[...].astype(jnp.float32)
    low = jnp.where(x == 0, near_sum, far_sum)
    high = jnp.where(x == 0, far_sum, near_sum)
    for f in range(2):
        lanes = slice(128 * f, 128 * f + 128)
        out[f, :, :, 0:128] = (low[..., lanes] + bias[:, 0:128][None]).astype(jnp.bfloat16)
        out[f, :, :, 128:256] = (high[..., lanes] + bias[:, 128:256][None]).astype(jnp.bfloat16)


def exchanged(block, k, j):
    tms = lax.axis_size("tm")
    tiles = lax.axis_size("tile")
    route = [(t * tms + m, (t ^ k) * tms + (m ^ j)) for t in range(tiles) for m in range(tms)]
    return lax.ppermute(block, ("tile", "tm"), route)


def across(block, j):
    route = [(2 * m + c, 2 * (m ^ j) + (1 - c)) for m in range(2) for c in range(2)]
    return lax.ppermute(block, ("tm", "ch"), route)


def resident_plan(latent, norm_gain, norm_shift, kernel, conv_bias, blend_profile):
    bf16, f32 = jnp.bfloat16, jnp.float32
    z, x, c = lax.axis_index("tile"), lax.axis_index("tm"), lax.axis_index("ch")
    pos = jnp.stack([z, x]).astype(jnp.int32)
    block = jax.ShapeDtypeStruct((8, 16, 128), bf16)
    wide = jax.ShapeDtypeStruct((8, 16, 256), bf16)

    def quarter(core, frame_block):
        start = core * 256 + frame_block * 128
        return lax.dynamic_slice_in_dim(kernel, start, 128, axis=4)

    quarters = (quarter(c, x), quarter(1 - c, x), quarter(c, 1 - x), quarter(1 - c, 1 - x))
    latent, quarters = lax.optimization_barrier((latent, quarters))
    same = quarters[0]
    other = across(quarters[1], 0)
    same_far = exchanged(quarters[2], 0, 1)
    other_far = across(quarters[3], 1)
    packed = call(pack_body, [block] * 4, [pltpu.VMEM((4, 8, 16, 128), bf16)])(pos, latent)
    near = [packed[0]] + [exchanged(packed[k], k, 0) for k in (1, 2, 3)]
    same_far, near[3] = lax.optimization_barrier((same_far, near[3]))
    far = [exchanged(part, 0, 1) for part in near]
    matrix = jax.ShapeDtypeStruct((TAPS, 768, 256), bf16)
    diag, lower = call(weights_body, [matrix] * 2)(pos, same, other, same_far, other_far)

    def lanes_of(vector):
        part = lax.dynamic_slice_in_dim(vector, z * 64, 64)
        return jnp.concatenate([part, part])[None]

    acts = call(
        norm_body,
        jax.ShapeDtypeStruct((2, 8, 96, 128), bf16),
        [pltpu.VMEM((2, 4, 8, 16, 128), bf16), pltpu.VMEM((2, 8, 72, 128), f32)],
    )(pos, lanes_of(norm_gain), lanes_of(norm_shift), *[near[k] for k in NORM], *[far[k] for k in NORM])
    sibling = lax.ppermute(acts, "ch", [(0, 1), (1, 0)])

    offsets = jnp.arange(2 * RIM, dtype=jnp.int32)
    ramps = ramp_weight(blend_profile[:3, None], offsets[None, :], RIM)
    blend = jnp.broadcast_to(ramps[:, :, None], (3, 2 * RIM, 256))
    *sends, kept, leaving = call(
        conv_body,
        [wide] * 4 + [jax.ShapeDtypeStruct((2, 8, 16, 256), t) for t in (f32, bf16)],
        [
            pltpu.VMEM((2, 960, 768), bf16),
            pltpu.VMEM((8, 72, 256), f32),
            pltpu.VMEM((2, 4, 8, 16, 256), f32),
        ],
    )(pos, acts, sibling, diag, lower, blend)
    came = exchanged(leaving, 1, 0)
    came, sends[0] = lax.optimization_barrier((came, sends[0]))
    own, leaving = call(add_body, [jax.ShapeDtypeStruct(wide.shape, f32), wide])(pos, kept, came)
    same = exchanged(leaving, 2, 0)
    far = [exchanged(sends[k], k, 1) for k in (3, 2, 0, 1)]
    return call(join_body, jax.ShapeDtypeStruct(latent.shape, bf16))(
        pos, conv_bias[None], own, same, *far
    )


def solution(mesh):
    in_specs = (
        P(("grp", "tm"), None, "tile", "ch"),
        P("ch"),
        P("ch"),
        P(None, None, None, ("ch", "tile", "tm"), None),
        P("ch"),
        P(),
    )
    out_specs = P(("grp", "tm"), None, "tile", "ch")

    def on_device(latent, norm_gain, norm_shift, kernel, conv_bias, blend_profile):
        plan = resident_plan if resident_fits(mesh.shape, latent, kernel) else gathered_plan
        return plan(latent, norm_gain, norm_shift, kernel, conv_bias, blend_profile)

    return jax.shard_map(
        on_device, mesh=mesh, in_specs=in_specs, out_specs=out_specs, check_vma=False
    )
```
